128 devices in a mesh: shot: 8 (over y, z_hi), gx: 16 (over z_lo, x, core).
Axes of the slice: x: 4, y: 4, z: 4 (z_hi: 2, z_lo: 2; z = z_hi * 2 + z_lo), core: 2. Of those that a mesh axis runs over, the one named last changes fastest.
Arguments:
- courant: float32 [128, 64, 256], P('gx'), may hold values from 0.08 to 0.3
- absorb: int32 [6], replicated, may hold values from 4 to 11
- model_image: float32 [128, 64, 256], P('gx'), may hold values from -6 to 6
- direction: float32 [128, 64, 256], P('gx'), may hold values from -6 to 6
- back_prev: float32 [16, 128, 64, 256], P('shot', 'gx'), may hold values from -12 to 12
- back_now: float32 [16, 128, 64, 256], P('shot', 'gx'), may hold values from -12 to 12
- scat_prev: float32 [16, 128, 64, 256], P('shot', 'gx'), may hold values from -12 to 12
- scat_now: float32 [16, 128, 64, 256], P('shot', 'gx'), may hold values from -12 to 12
- back_end: float32 [16, 128, 64, 256], P('shot', 'gx'), may hold values from -12 to 12
- back_before_end: float32 [16, 128, 64, 256], P('shot', 'gx'), may hold values from -12 to 12
- back_band: float32 [16, 4, 128, 64, 256], P('shot', None, 'gx'), may hold values from -12 to 12
- src_pos: int32 [16, 64, 3], P('shot'), may hold values from 0 to 255, as said below
- wavelet: float32 [16, 4], P('shot'), may hold values from -30 to 30
- rec_pos: int32 [16, 2048, 3], P('shot', 'gx'), may hold values from 0 to 255, as said below
- residual: float32 [16, 4, 2048], P('shot', None, 'gx'), may hold values from -6 to 6
- grad_norm: float32 [1], replicated, may hold values from 131072 to 786432
Outputs:
- image_new: float32 [128, 64, 256], P('gx')
- direction_new: float32 [128, 64, 256], P('gx')
- residual_new: float32 [16, 4, 2048], P('shot', None, 'gx')
The draws below stay inside these ranges and needn't reach their ends.
Inputs may be any that keep to these rules, and one draw needn't show every extreme that they name: `src_pos`: each entry is a grid cell: 0 <= x < 128, 0 <= y < 64, 0 <= z < 256. Each entry is a grid cell with 0 <= y < 64 and 0 <= z < 256; receiver j lies at an x between (j // 128) * 8 and (j // 128) * 8 + 7; every shot group uses the same receiver cells (rec_pos[s] is the same for every s).
All inputs are finite; a program needn't handle non-finite values.
Results may differ from the reference program's by a relative error of at most 0.00027.
Values sent between devices are 32-bit elements; how exact they have to be, the bound alone decides.
A program may use at most 128 MiB of HBM per device.

```python
import math
import jax
import jax.numpy as jnp
from jax import lax

CX = 8
NY = 64
NZ = 256
REC_DEV = 128
SRC = 64
STEPS = 4
SHOTS = 16
NX = 128
NREC = 2048


def level_scale():
    shot_part = jnp.arange(SHOTS, dtype=jnp.float32) / max(SHOTS - 1, 1)
    slab_part = jnp.arange(NX, dtype=jnp.float32) / max(NX - 1, 1)
    shot_gain = jnp.exp(0.5 * jnp.log(3.0) * shot_part)
    slab_gain = jnp.exp(0.5 * jnp.log(3.0) * slab_part)
    return shot_gain[:, None, None, None] * slab_gain[None, :, None, None]


def level_values(key, grid_shape):
    values = jax.random.truncated_normal(key, -4.0, 4.0, grid_shape, jnp.float32)
    return values


def level_field(key, tag):
    key = jax.random.fold_in(key, tag)
    return level_values(key, (SHOTS, NX, NY, NZ)) * level_scale()


def rebuild_field(key, tag):
    values = level_field(key, tag)
    return values


def draw_back_prev(key, part):
    return level_field(key, 11)


def draw_back_now(key, part):
    return level_field(key, 12)


def draw_scat_prev(key, part):
    return level_field(key, 13)


def draw_scat_now(key, part):
    return level_field(key, 14)


def draw_back_end(key, part):
    return rebuild_field(key, 15)


def draw_back_before_end(key, part):
    return rebuild_field(key, 16)


def draw_back_band(key, part):
    key = jax.random.fold_in(key, 17)
    values = level_values(key, (SHOTS, STEPS, NX, NY, NZ)) * level_scale()[:, None]
    return values


def draw_src_pos(key, part):
    key = jax.random.fold_in(key, 21)
    key_x, key_y, key_z = jax.random.split(key, 3)
    place_x = jax.random.randint(key_x, (SHOTS, SRC, 1), 0, NX, dtype=jnp.int32)
    place_y = jax.random.randint(key_y, (SHOTS, SRC, 1), 0, NY, dtype=jnp.int32)
    place_z = jax.random.randint(key_z, (SHOTS, SRC, 1), 0, NZ, dtype=jnp.int32)
    places = jnp.concatenate([place_x, place_y, place_z], axis=2).astype(jnp.int32)
    corner = jnp.array([NX - 1, NY - 1, NZ - 1], dtype=jnp.int32)
    return places.at[0, 0].set(corner)


def draw_rec_pos(key, part):
    key = jax.random.fold_in(key, 22)
    key_x, key_y, key_z = jax.random.split(key, 3)
    block_id = jnp.arange(NREC, dtype=jnp.int32) // REC_DEV
    place_x = block_id * CX + jax.random.randint(key_x, (NREC,), 0, CX, dtype=jnp.int32)
    place_y = jax.random.randint(key_y, (NREC,), 0, NY, dtype=jnp.int32)
    place_z = jax.random.randint(key_z, (NREC,), 0, NZ, dtype=jnp.int32)
    places = jnp.stack([place_x, place_y, place_z], axis=1).astype(jnp.int32)
    corner = jnp.array([NX - 1, NY - 1, NZ - 1], dtype=jnp.int32)
    places = places.at[NREC - 1].set(corner)
    return jnp.broadcast_to(places[None], (SHOTS, NREC, 3)).astype(jnp.int32)


def touch_ends(drawn, key, low, top_value):
    shape = drawn.shape
    spot = [jax.random.randint(jax.random.fold_in(key, axis), (), 0, shape[axis]) for axis in range(len(shape))]
    drawn = drawn.at[tuple(spot)].set(low)
    longest = shape.index(max(shape))
    spot[longest] = (spot[longest] + 1) % shape[longest]
    return drawn.at[tuple(spot)].set(top_value)


def block_scale(stream_key, shape, shards, low, largest):
    def one(dim, shards_of):
        draws = jax.random.uniform(jax.random.fold_in(jax.random.fold_in(stream_key, 6), dim), (shards_of,), jnp.float32, low / len(shards), largest / len(shards))
        return jnp.repeat(jnp.exp(draws), shape[dim] // shards_of).reshape((-1,) + (1,) * (len(shape) - dim - 1))

    factor_of = one(*shards[0])
    for cut in shards[1:]:
        factor_of = factor_of * one(*cut)
    return factor_of


def normal_values(own_key, shape, width, bound, cuts=(), kind=jnp.bfloat16):
    entries = width * jax.random.normal(own_key, shape, jnp.float32)
    if cuts:
        entries = entries * block_scale(own_key, shape, cuts, -0.22, 0.18)
    return jnp.clip(entries, -bound, bound).astype(kind)


def setup_inputs(seed: int = 0) -> dict:
    seeds = jax.random.split(jax.random.key(seed), 17)
    courant = jnp.clip(jnp.exp(math.log(0.3) - 1.3217559 * jax.random.uniform(seeds[0], (NX, NY, NZ), jnp.float32) ** block_scale(seeds[0], (NX, NY, NZ), ((0, 16),), -0.2, 0.2)), 0.08, 0.3)
    absorb = touch_ends(jax.random.randint(seeds[1], (6,), 4, 12), jax.random.fold_in(seeds[1], 1), 4, 11).astype(jnp.int32)
    model_image = normal_values(seeds[2], (NX, NY, NZ), 1.0, 6.0, ((0, 16),), jnp.float32)
    direction = normal_values(seeds[3], (NX, NY, NZ), 1.0, 6.0, ((0, 16),), jnp.float32)
    back_prev = draw_back_prev(jax.random.fold_in(seeds[16], 71), 0)
    back_now = draw_back_now(jax.random.fold_in(seeds[16], 71), 0)
    scat_prev = draw_scat_prev(jax.random.fold_in(seeds[16], 71), 0)
    scat_now = draw_scat_now(jax.random.fold_in(seeds[16], 71), 0)
    back_end = draw_back_end(jax.random.fold_in(seeds[16], 71), 0)
    back_before_end = draw_back_before_end(jax.random.fold_in(seeds[16], 71), 0)
    back_band = draw_back_band(jax.random.fold_in(seeds[16], 71), 0)
    src_pos = draw_src_pos(jax.random.fold_in(seeds[16], 71), 0)
    wavelet = normal_values(seeds[12], (SHOTS, STEPS), 6.0, 30.0, ((0, 8),), jnp.float32)
    rec_pos = draw_rec_pos(jax.random.fold_in(seeds[16], 71), 0)
    residual = normal_values(seeds[14], (SHOTS, STEPS, NREC), 1.0, 6.0, ((0, 8), (2, 16)), jnp.float32)
    grad_norm = jnp.clip(jnp.exp(jax.random.uniform(seeds[15], (1,), jnp.float32, math.log(131072.0), math.log(786432.0))), 131072.0, 786432.0)
    return dict(courant=courant, absorb=absorb, model_image=model_image, direction=direction, back_prev=back_prev, back_now=back_now, scat_prev=scat_prev, scat_now=scat_now, back_end=back_end, back_before_end=back_before_end, back_band=back_band, src_pos=src_pos, wavelet=wavelet, rec_pos=rec_pos, residual=residual, grad_norm=grad_norm)


damp_peak = 0.4
tiny = 1e-6


def laplace(values):
    padded = jnp.pad(values, 1)
    nearby = padded[2:, 1:-1, 1:-1] + padded[:-2, 1:-1, 1:-1]
    nearby = nearby + padded[1:-1, 2:, 1:-1] + padded[1:-1, :-2, 1:-1]
    nearby = nearby + padded[1:-1, 1:-1, 2:] + padded[1:-1, 1:-1, :-2]
    return nearby - 6.0 * values


def profile(position, extent, low_width, high_width):
    upper_gap = extent - 1 - position
    low_float = low_width.astype(jnp.float32)
    high_float = high_width.astype(jnp.float32)
    near_low = jnp.where(position < low_width, ((low_width - position).astype(jnp.float32) / low_float) ** 2, 0.0)
    near_high = jnp.where(upper_gap < high_width, ((high_width - upper_gap).astype(jnp.float32) / high_float) ** 2, 0.0)
    return damp_peak * (near_low + near_high), (position < low_width) | (upper_gap < high_width)


def layers(absorb, position_x, extent_x, extent_y, extent_z):
    damp_x, layer_x = profile(position_x, extent_x, absorb[0], absorb[1])
    damp_y, layer_y = profile(jnp.arange(extent_y, dtype=jnp.int32), extent_y, absorb[2], absorb[3])
    damp_z, layer_z = profile(jnp.arange(extent_z, dtype=jnp.int32), extent_z, absorb[4], absorb[5])
    damping = damp_x[:, None, None] + damp_y[None, :, None] + damp_z[None, None, :]
    in_layer = layer_x[:, None, None] | layer_y[None, :, None] | layer_z[None, None, :]
    return damping, in_layer


def inject(amounts, flat_index, grid_shape):
    buffer = jnp.zeros(grid_shape, jnp.float32).reshape(-1)
    return buffer.at[flat_index].add(amounts).reshape(grid_shape)


def forward_traces(courant, damping, direction, back_prev, back_now, scat_prev, scat_now, src_flat, wave_row, rec_flat):
    trace_list = []
    for time_step in range(STEPS):
        source_term = inject(jnp.broadcast_to(wave_row[time_step], src_flat.shape), src_flat, courant.shape)
        back_next = (2.0 * back_now - (1.0 - damping) * back_prev + courant * laplace(back_now) + source_term) / (1.0 + damping)
        back_accel = back_next - 2.0 * back_now + back_prev
        scat_next = (2.0 * scat_now - (1.0 - damping) * scat_prev + courant * laplace(scat_now) - courant * direction * back_accel) / (1.0 + damping)
        trace_list.append(scat_next.reshape(-1)[rec_flat])
        back_prev, back_now = back_now, back_next
        scat_prev, scat_now = scat_now, scat_next
    return jnp.stack(trace_list)


def migrate(courant, damping, in_layer, back_upper, back_middle, band, src_flat, wave_row, rec_flat, drive_rows):
    adj_older = jnp.zeros_like(back_middle)
    adj_newer = jnp.zeros_like(back_middle)
    image_sum = jnp.zeros_like(back_middle)
    for time_step in reversed(range(STEPS)):
        source_term = inject(jnp.broadcast_to(wave_row[time_step], src_flat.shape), src_flat, courant.shape)
        rebuilt = 2.0 * back_middle - back_upper + courant * laplace(back_middle) + source_term
        back_lower = jnp.where(in_layer, band[time_step], rebuilt)
        back_accel = back_upper - 2.0 * back_middle + back_lower
        adj_now = (2.0 * adj_newer - (1.0 - damping) * adj_older + courant * laplace(adj_newer) + inject(drive_rows[time_step], rec_flat, courant.shape)) / (1.0 + damping)
        image_sum = image_sum - courant * back_accel * adj_now
        adj_older, adj_newer = adj_newer, adj_now
        back_upper, back_middle = back_middle, back_lower
    return image_sum


def reference(courant, absorb, model_image, direction, back_prev, back_now, scat_prev, scat_now, back_end, back_before_end, back_band, src_pos, wavelet, rec_pos, residual, grad_norm):
    damping, in_layer = layers(absorb, jnp.arange(NX, dtype=jnp.int32), NX, NY, NZ)
    src_flat = ((src_pos[..., 0] * NY + src_pos[..., 1]) * NZ + src_pos[..., 2]).astype(jnp.int32)
    rec_flat = ((rec_pos[..., 0] * NY + rec_pos[..., 1]) * NZ + rec_pos[..., 2]).astype(jnp.int32)

    def record(shot_items):
        return forward_traces(courant, damping, direction, shot_items[0], shot_items[1], shot_items[2], shot_items[3], shot_items[4], shot_items[5], shot_items[6])

    all_traces = lax.map(record, (back_prev, back_now, scat_prev, scat_now, src_flat, wavelet, rec_flat))
    energy = jnp.sum(all_traces * all_traces)
    step_size = grad_norm[0] / (energy + tiny)
    residual_new = residual - step_size * all_traces

    def accumulate(gradient, shot_items):
        term = migrate(courant, damping, in_layer, shot_items[0], shot_items[1], shot_items[2], shot_items[3], shot_items[4], shot_items[5], shot_items[6])
        return gradient + term, None

    gradient, unused = lax.scan(accumulate, jnp.zeros((NX, NY, NZ), jnp.float32), (back_end, back_before_end, back_band, src_flat, wavelet, rec_flat, residual_new))
    grad_energy = jnp.sum(gradient * gradient)
    conj_ratio = grad_energy / grad_norm[0]
    return model_image + step_size * direction, gradient + conj_ratio * direction, residual_new
```

```python
import functools

import jax
import jax.numpy as jnp
from jax import lax
from jax.experimental import pallas as pl
from jax.experimental.pallas import tpu as pltpu
from jax.sharding import PartitionSpec as P

damp_peak = 0.4
tiny = 1e-6
CX, NY, NZ = 8, 64, 256
NS, STEPS, REC, SRC = 2, 4, 128, 64
PY = 80
HALF = 128
MESH = pl.DeviceIdType.MESH
f32 = jnp.float32
bf16 = jnp.bfloat16


def split2(v):
    hi = v.astype(bf16)
    lo = (v - hi.astype(f32)).astype(bf16)
    return hi, lo


def profile(pos, extent, low, high):
    gap = extent - 1 - pos
    low_f = low.astype(f32)
    high_f = high.astype(f32)
    near_low = jnp.where(pos < low, ((low - pos).astype(f32) / low_f) ** 2, 0.0)
    near_high = jnp.where(gap < high, ((high - gap).astype(f32) / high_f) ** 2, 0.0)
    return damp_peak * (near_low + near_high)


def kernel(
    n_shot,
    n_gx,
    courant_h,
    direction_h,
    back_prev_h,
    back_now_h,
    scat_prev_h,
    scat_now_h,
    back_end_h,
    back_before_h,
    band_h,
    absorb,
    wavelet,
    grad_norm,
    src_pos,
    rec_pos,
    residual,
    grad_o,
    resid_o,
    scal_o,
    F0,
    F1,
    U0,
    U1,
    band,
    c0,
    dirv,
    ca,
    cb,
    cc,
    inv,
    cnt,
    rowhot,
    zt,
    zh2,
    tr,
    amt,
    img,
    rs,
    ebuf,
    eslot_s,
    eslot_g,
    ld_sem,
    f_send,
    f_recv,
    u_send,
    u_recv,
    e_send_s,
    e_recv_s,
    e_send_g,
    e_recv_g,
    g_send,
    g_recv,
):
    me_s = lax.axis_index("shot")
    me_g = lax.axis_index("gx")
    F = (F0, F1)
    U = (U0, U1)

    loads = {}

    def load(name, src, dst, k):
        c = pltpu.make_async_copy(src, dst, ld_sem.at[k])
        c.start()
        loads.setdefault(name, []).append(c)

    k = 0
    for z in range(2):
        zs = pl.ds(z * HALF, HALF)
        load("coef", courant_h.at[:, :, zs], c0.at[z], k)
        k += 1
    fields = (
        ("f0", 0, 0, back_now_h),
        ("f0", 0, 1, scat_now_h),
        ("f0", 0, 2, back_before_h),
        ("f1", 1, 0, back_prev_h),
        ("f1", 1, 1, scat_prev_h),
        ("f1", 1, 2, back_end_h),
    )
    for name, b, f, src in fields:
        for z in range(2):
            zs = pl.ds(z * HALF, HALF)
            load(
                name,
                src.at[:, :, :, zs],
                F[b].at[f, :, z, pl.ds(1, CX), pl.ds(8, NY), :],
                k,
            )
            k += 1
    for z in range(2):
        zs = pl.ds(z * HALF, HALF)
        load("f1", direction_h.at[:, :, zs], dirv.at[z], k)
        k += 1
    load("f1", band_h, band, k)

    zero8 = jnp.zeros((8, HALF), f32)
    zero64 = jnp.zeros((NY, HALF), f32)

    def zero_pads(ref, lead):
        def one(p, carry):
            for idx in lead:
                ref[idx + (p, pl.ds(0, 8), slice(None))] = zero8
                ref[idx + (p, pl.ds(72, 8), slice(None))] = zero8
            return carry

        lax.fori_loop(0, CX + 2, one, 0)
        for idx in lead:
            for p in (0, CX + 1):
                ref[idx + (p, pl.ds(8, NY), slice(None))] = zero64

    lead3 = [(f, s, z) for f in range(3) for s in range(NS) for z in range(2)]
    lead2 = [(s, z) for s in range(NS) for z in range(2)]
    for b in range(2):
        zero_pads(F[b], lead3)
        zero_pads(U[b], lead2)

    bar = pltpu.get_barrier_semaphore()
    for d in range(1, n_gx):
        pl.semaphore_signal(
            bar, inc=1, device_id=(me_s, lax.rem(me_g + d, n_gx)), device_id_type=MESH
        )
    for d in range(1, n_shot):
        pl.semaphore_signal(
            bar, inc=1, device_id=(lax.rem(me_s + d, n_shot), me_g), device_id_type=MESH
        )
    pl.semaphore_wait(bar, n_gx - 1 + n_shot - 1)

    def face(buf, lead, send, recv, side):
        src_p, dst_p = (1, CX + 1) if side == 0 else (CX, 0)
        nb = me_g - 1 if side == 0 else me_g + 1
        return pltpu.make_async_remote_copy(
            src_ref=buf.at[lead + (src_p, pl.ds(8, NY), slice(None))],
            dst_ref=buf.at[lead + (dst_p, pl.ds(8, NY), slice(None))],
            send_sem=send.at[side],
            recv_sem=recv.at[side],
            device_id=(me_s, nb),
            device_id_type=MESH,
        )

    has_left = me_g > 0
    has_right = me_g < n_gx - 1

    def send_faces(buf, lead, send, recv):
        @pl.when(has_left)
        def _():
            face(buf, lead, send, recv, 0).start()

        @pl.when(has_right)
        def _():
            face(buf, lead, send, recv, 1).start()

    def wait_recv(buf, lead, send, recv):
        @pl.when(has_right)
        def _():
            face(buf, lead, send, recv, 0).wait_recv()

        @pl.when(has_left)
        def _():
            face(buf, lead, send, recv, 1).wait_recv()

    def wait_send(buf, lead, send, recv):
        @pl.when(has_left)
        def _():
            face(buf, lead, send, recv, 0).wait_send()

        @pl.when(has_right)
        def _():
            face(buf, lead, send, recv, 1).wait_send()

    all3 = (slice(None), slice(None), slice(None))
    all2 = (slice(None), slice(None))

    for c in loads["f0"]:
        c.wait()
    send_faces(F0, all3, f_send.at[0], f_recv.at[0])

    lane128 = lax.broadcasted_iota(jnp.int32, (REC, REC), 1)
    sub128 = lax.broadcasted_iota(jnp.int32, (REC, REC), 0)

    def to_row(col, n):
        eye = (
            lax.broadcasted_iota(jnp.int32, (n, n), 0)
            == lax.broadcasted_iota(jnp.int32, (n, n), 1)
        )
        return jnp.sum(jnp.where(eye, col.astype(f32), 0.0), axis=0, keepdims=True)

    rec = rec_pos[0]
    rec_row_col = (rec[:, 0:1] - me_g * CX) * NY + rec[:, 1:2]
    rec_z_col = rec[:, 2:3]
    rec_row = to_row(rec_row_col, REC).astype(jnp.int32)
    rec_z = to_row(rec_z_col, REC).astype(jnp.int32)
    rowhot[...] = jnp.where(
        lax.broadcasted_iota(jnp.int32, (CX * NY, REC), 0) == rec_row, 1.0, 0.0
    )
    zt[...] = jnp.where(
        lax.broadcasted_iota(jnp.int32, (NZ, REC), 0) == rec_z, 1.0, 0.0
    ).astype(bf16)
    zhot = jnp.where(
        lax.broadcasted_iota(jnp.int32, (REC, NZ), 1) == rec_z_col, 1.0, 0.0
    ).astype(bf16)
    zh2[pl.ds(0, REC), :] = zhot
    zh2[pl.ds(REC, REC), :] = zhot

    for c in loads["coef"]:
        c.wait()

    nx = n_gx * CX
    damp_z = [
        profile(
            lax.broadcasted_iota(jnp.int32, (8, HALF), 1) + z * HALF, NZ, absorb[4], absorb[5]
        )
        for z in range(2)
    ]

    def coef(i, carry):
        p = i // 8
        y8 = pl.multiple_of((i % 8) * 8, 8)
        ys = pl.ds(y8, 8)
        pos_x = jnp.full((8, HALF), me_g * CX + p, jnp.int32)
        damp_xy = profile(pos_x, nx, absorb[0], absorb[1]) + profile(
            lax.broadcasted_iota(jnp.int32, (8, HALF), 0) + y8, NY, absorb[2], absorb[3]
        )
        for z in range(2):
            damping = damp_xy + damp_z[z]
            c = c0[z, p, ys, :]
            iv = 1.0 / (1.0 + damping)
            inv[z, p, ys, :] = iv
            ca[z, p, ys, :] = (2.0 - 6.0 * c) * iv
            cb[z, p, ys, :] = (1.0 - damping) * iv
            cc[z, p, ys, :] = c * iv
        return carry

    lax.fori_loop(0, CX * 8, coef, 0)

    for s in range(NS):
        src = src_pos[s]
        s_row = to_row((src[:, 0:1] - me_g * CX) * NY + src[:, 1:2], SRC).astype(jnp.int32)
        s_zhot = jnp.where(
            lax.broadcasted_iota(jnp.int32, (SRC, NZ), 1) == src[:, 2:3], 1.0, 0.0
        ).astype(bf16)

        def count(p, carry):
            rows = lax.broadcasted_iota(jnp.int32, (NY, SRC), 0) + p * NY
            hot = jnp.where(rows == s_row, 1.0, 0.0).astype(bf16)
            n = jnp.dot(hot, s_zhot, preferred_element_type=f32)
            for z in range(2):
                cnt[s, z, p] = n[:, z * HALF : (z + 1) * HALF] * inv[z, p]
            return carry

        lax.fori_loop(0, CX, count, 0)

    for c in loads["f1"]:
        c.wait()

    lane = lax.broadcasted_iota(jnp.int32, (8, HALF), 1)
    first = lane == 0
    last = lane == HALF - 1

    def neighbours(ref, lead, p, y8):
        ys = pl.ds(pl.multiple_of(y8 + 8, 8), 8)
        mid = [ref[lead + (z, p, ys, slice(None))] for z in range(2)]
        sums = []
        right = [pltpu.roll(m, 1, 1) for m in mid]
        left = [pltpu.roll(m, HALF - 1, 1) for m in mid]
        low = [jnp.where(first, 0.0, right[0]), jnp.where(first, right[0], right[1])]
        high = [jnp.where(last, left[1], left[0]), jnp.where(last, 0.0, left[1])]
        for z in range(2):
            t = ref[lead + (z, p + 1, ys, slice(None))] + ref[lead + (z, p - 1, ys, slice(None))]
            t = t + (
                ref[lead + (z, p, pl.ds(y8 + 9, 8), slice(None))]
                + ref[lead + (z, p, pl.ds(y8 + 7, 8), slice(None))]
            )
            sums.append(t + (low[z] + high[z]))
        return mid, sums

    def forward(n, p, y8):
        now, nxt = F[n % 2], F[(n + 1) % 2]
        q = p - 1
        ys = pl.ds(y8, 8)
        ysp = pl.ds(pl.multiple_of(y8 + 8, 8), 8)
        a = [ca[z, q, ys, :] for z in range(2)]
        b = [cb[z, q, ys, :] for z in range(2)]
        c = [cc[z, q, ys, :] for z in range(2)]
        cr = [c0[z, q, ys, :] for z in range(2)]
        di = [dirv[z, q, ys, :] for z in range(2)]
        for s in range(NS):
            k = [cnt[s, z, q, ys, :] for z in range(2)]
            w = wavelet[s, n]
            wr = wavelet[s, STEPS - 1 - n]
            mid, sums = neighbours(now, (0, s), p, y8)
            acc = []
            for z in range(2):
                old = nxt[0, s, z, p, ysp, :]
                new = a[z] * mid[z] - b[z] * old + c[z] * sums[z] + w * k[z]
                nxt[0, s, z, p, ysp, :] = new
                acc.append((new - mid[z]) - (mid[z] - old))
            mid, sums = neighbours(now, (1, s), p, y8)
            for z in range(2):
                old = nxt[1, s, z, p, ysp, :]
                nxt[1, s, z, p, ysp, :] = (
                    a[z] * mid[z] - b[z] * old + c[z] * (sums[z] - di[z] * acc[z])
                )
            mid, sums = neighbours(now, (2, s), p, y8)
            for z in range(2):
                zs = pl.ds(z * HALF, HALF)
                old = nxt[2, s, z, p, ysp, :]
                new = a[z] * mid[z] - b[z] * old + c[z] * sums[z] + wr * k[z]
                kept = band[s, STEPS - 1 - n, q, ys, zs]
                new = jnp.where(b[z] < 1.0, kept, new)
                nxt[2, s, z, p, ysp, :] = new
                band[s, STEPS - 1 - n, q, ys, zs] = cr[z] * ((new - mid[z]) - (mid[z] - old))

    def gather(n):
        ref = F[(n + 1) % 2]
        zero = jnp.zeros((NY, REC), f32)

        def one(p, carry):
            hot = rowhot[pl.ds(pl.multiple_of(p * NY, NY), NY), :]
            out = []
            for s in range(NS):
                v = jnp.concatenate(
                    [ref[1, s, z, p + 1, pl.ds(8, NY), :] for z in range(2)], axis=1
                )
                hi, lo = split2(v)
                g = jnp.dot(hi, zt[...], preferred_element_type=f32) + jnp.dot(
                    lo, zt[...], preferred_element_type=f32
                )
                out.append(carry[s] + hot * g)
            return tuple(out)

        got = lax.fori_loop(0, CX, one, (zero, zero))
        for s in range(NS):
            tr[pl.ds(s * STEPS + n, 1), :] = jnp.sum(got[s], axis=0, keepdims=True)

    for n in range(STEPS):
        wait_recv(F[n % 2], all3, f_send.at[n], f_recv.at[n])
        if n > 0:
            wait_send(F[(n + 1) % 2], all3, f_send.at[n - 1], f_recv.at[n - 1])

        def edge(i, carry):
            forward(n, 1 + (CX - 1) * (i // 8), pl.multiple_of((i % 8) * 8, 8))
            return carry

        lax.fori_loop(0, 16, edge, 0)
        if n < STEPS - 1:
            send_faces(F[(n + 1) % 2], all3, f_send.at[n + 1], f_recv.at[n + 1])

        def inner(i, carry):
            forward(n, 2 + i // 8, pl.multiple_of((i % 8) * 8, 8))
            return carry

        lax.fori_loop(0, (CX - 2) * 8, inner, 0)
        gather(n)
    wait_send(F[1], all3, f_send.at[STEPS - 1], f_recv.at[STEPS - 1])

    def allreduce(value, r):
        ebuf[r, 0] = value
        eslot_s[r, me_s] = value
        copies = []
        for d in range(1, n_shot):
            copies.append(
                pltpu.make_async_remote_copy(
                    src_ref=ebuf.at[r, 0],
                    dst_ref=eslot_s.at[r, me_s],
                    send_sem=e_send_s.at[r, d],
                    recv_sem=e_recv_s.at[r, d],
                    device_id=(lax.rem(me_s + d, n_shot), me_g),
                    device_id_type=MESH,
                )
            )
        for c in copies:
            c.start()
        for c in copies:
            c.wait_recv()
        total = eslot_s[r, 0]
        for d in range(1, n_shot):
            total = total + eslot_s[r, d]
        ebuf[r, 1] = total
        eslot_g[r, me_g] = total
        second = []
        for d in range(1, n_gx):
            second.append(
                pltpu.make_async_remote_copy(
                    src_ref=ebuf.at[r, 1],
                    dst_ref=eslot_g.at[r, me_g],
                    send_sem=e_send_g.at[r, d],
                    recv_sem=e_recv_g.at[r, d],
                    device_id=(me_s, lax.rem(me_g + d, n_gx)),
                    device_id_type=MESH,
                )
            )
        for c in second:
            c.start()
        for c in second:
            c.wait_recv()
        total = eslot_g[r, 0]
        for d in range(1, n_gx):
            total = total + eslot_g[r, d]
        for c in copies + second:
            c.wait_send()
        return jnp.sum(total)

    t = tr[...]
    energy = allreduce(t * t, 0)
    gn = jnp.full((8, HALF), grad_norm[0], f32)
    step = gn / (jnp.full((8, HALF), energy, f32) + tiny)
    for s in range(NS):
        r = residual[s] - step[0:STEPS] * t[s * STEPS : (s + 1) * STEPS]
        resid_o[s] = r
        amt[pl.ds(s * STEPS, STEPS), :] = r

    def adjoint(m, p, y8, force):
        now, nxt = U[(m + 1) % 2], U[m % 2]
        q = p - 1
        ys = pl.ds(y8, 8)
        ysp = pl.ds(pl.multiple_of(y8 + 8, 8), 8)
        n = STEPS - 1 - m
        pic = [None, None]
        for s in range(NS):
            if m > 0:
                mid, sums = neighbours(now, (s,), p, y8)
            for z in range(2):
                zs = pl.ds(z * HALF, HALF)
                u = inv[z, q, ys, :] * force[s, ys, zs]
                if m > 0:
                    u = u + ca[z, q, ys, :] * mid[z] + cc[z, q, ys, :] * sums[z]
                if m > 1:
                    u = u - cb[z, q, ys, :] * nxt[s, z, p, ysp, :]
                if m < STEPS - 1:
                    nxt[s, z, p, ysp, :] = u
                part = band[s, n, q, ys, zs] * u
                pic[z] = part if s == 0 else pic[z] + part
        for z in range(2):
            zs = pl.ds(z * HALF, HALF)
            if m == 0:
                img[q, ys, zs] = -pic[z]
            else:
                img[q, ys, zs] = img[q, ys, zs] - pic[z]

    force = rs

    def adjoint_plane(m, p):
        n = STEPS - 1 - m
        q = p - 1
        hot = rowhot[pl.ds(pl.multiple_of(q * NY, NY), NY), :]
        for s in range(NS):
            hi, lo = split2(amt[pl.ds(s * STEPS + n, 1), :])
            both = jnp.concatenate(
                [(hot * hi.astype(f32)).astype(bf16), (hot * lo.astype(f32)).astype(bf16)],
                axis=1,
            )
            force[s] = jnp.dot(both, zh2[...], preferred_element_type=f32)

        def chunk(i, carry):
            adjoint(m, p, pl.multiple_of(i * 8, 8), force)
            return carry

        lax.fori_loop(0, 8, chunk, 0)

    for m in range(STEPS):
        if m > 0:
            wait_recv(U[(m + 1) % 2], all2, u_send.at[m - 1], u_recv.at[m - 1])
        if m > 1:
            wait_send(U[m % 2], all2, u_send.at[m - 2], u_recv.at[m - 2])

        def edge(i, carry):
            adjoint_plane(m, 1 + (CX - 1) * i)
            return carry

        lax.fori_loop(0, 2, edge, 0)
        if m < STEPS - 1:
            send_faces(U[m % 2], all2, u_send.at[m], u_recv.at[m])

        def inner(i, carry):
            adjoint_plane(m, 2 + i)
            return carry

        lax.fori_loop(0, CX - 2, inner, 0)
    wait_send(U[0], all2, u_send.at[STEPS - 2], u_recv.at[STEPS - 2])

    scatter = []
    for d in range(1, n_shot):
        to = lax.rem(me_s + d, n_shot)
        scatter.append(
            pltpu.make_async_remote_copy(
                src_ref=img.at[to],
                dst_ref=rs.at[NS + d - 1],
                send_sem=g_send.at[0, d],
                recv_sem=g_recv.at[0, d],
                device_id=(to, me_g),
                device_id_type=MESH,
            )
        )
    for c in scatter:
        c.start()
    for c in scatter:
        c.wait_recv()

    def add(i, carry):
        ys = pl.ds(pl.multiple_of(i * 8, 8), 8)
        g = img[me_s, ys, :]
        for d in range(1, n_shot):
            g = g + rs[NS + d - 1, ys, :]
        grad_o[me_s, ys, :] = g
        g = g * g
        return carry + (g[:, :HALF] + g[:, HALF:])

    part = lax.fori_loop(0, 8, add, jnp.zeros((8, HALF), f32))
    spread = []
    for d in range(1, n_shot):
        to = lax.rem(me_s + d, n_shot)
        spread.append(
            pltpu.make_async_remote_copy(
                src_ref=grad_o.at[me_s],
                dst_ref=grad_o.at[me_s],
                send_sem=g_send.at[1, d],
                recv_sem=g_recv.at[1, d],
                device_id=(to, me_g),
                device_id_type=MESH,
            )
        )
    for c in spread:
        c.start()
    grad_energy = allreduce(part, 1)
    ratio = jnp.full((8, HALF), grad_energy, f32) / gn
    scal_o[pl.ds(0, 8), :] = step
    scal_o[pl.ds(8, 8), :] = ratio
    for d in range(1, n_shot):
        came = lax.rem(me_s + n_shot - d, n_shot)
        pltpu.make_async_remote_copy(
            src_ref=grad_o.at[came],
            dst_ref=grad_o.at[came],
            send_sem=g_send.at[1, d],
            recv_sem=g_recv.at[1, d],
            device_id=(came, me_g),
            device_id_type=MESH,
        ).wait_recv()
    for c in scatter + spread:
        c.wait_send()


def per_device(
    n_shot,
    n_gx,
    courant,
    absorb,
    model_image,
    direction,
    back_prev,
    back_now,
    scat_prev,
    scat_now,
    back_end,
    back_before_end,
    back_band,
    src_pos,
    wavelet,
    rec_pos,
    residual,
    grad_norm,
):
    hbm = pl.BlockSpec(memory_space=pl.ANY)
    vmem = pl.BlockSpec(memory_space=pltpu.VMEM)
    smem = pl.BlockSpec(memory_space=pltpu.SMEM)
    slab = (2, CX, NY, HALF)
    dma = pltpu.SemaphoreType.DMA
    gradient, residual_new, scal = pl.pallas_call(
        functools.partial(kernel, n_shot, n_gx),
        out_shape=(
            jax.ShapeDtypeStruct((CX, NY, NZ), f32),
            jax.ShapeDtypeStruct((NS, STEPS, REC), f32),
            jax.ShapeDtypeStruct((16, HALF), f32),
        ),
        in_specs=[hbm] * 9 + [smem] * 3 + [vmem] * 3,
        out_specs=(vmem, vmem, vmem),
        scratch_shapes=[
            pltpu.VMEM((3, NS, 2, CX + 2, PY, HALF), f32),
            pltpu.VMEM((3, NS, 2, CX + 2, PY, HALF), f32),
            pltpu.VMEM((NS, 2, CX + 2, PY, HALF), f32),
            pltpu.VMEM((NS, 2, CX + 2, PY, HALF), f32),
            pltpu.VMEM((NS, STEPS, CX, NY, NZ), f32),
            pltpu.VMEM(slab, f32),
            pltpu.VMEM(slab, f32),
            pltpu.VMEM(slab, f32),
            pltpu.VMEM(slab, f32),
            pltpu.VMEM(slab, f32),
            pltpu.VMEM(slab, f32),
            pltpu.VMEM((NS,) + slab, f32),
            pltpu.VMEM((CX * NY, REC), f32),
            pltpu.VMEM((NZ, REC), bf16),
            pltpu.VMEM((2 * REC, NZ), bf16),
            pltpu.VMEM((NS * STEPS, REC), f32),
            pltpu.VMEM((NS * STEPS, REC), f32),
            pltpu.VMEM((CX, NY, NZ), f32),
            pltpu.VMEM((NS + n_shot - 1, NY, NZ), f32),
            pltpu.VMEM((2, 2, 8, HALF), f32),
            pltpu.VMEM((2, n_shot, 8, HALF), f32),
            pltpu.VMEM((2, n_gx, 8, HALF), f32),
            dma((17,)),
            dma((STEPS, 2)),
            dma((STEPS, 2)),
            dma((STEPS - 1, 2)),
            dma((STEPS - 1, 2)),
            dma((2, n_shot)),
            dma((2, n_shot)),
            dma((2, n_gx)),
            dma((2, n_gx)),
            dma((2, n_shot)),
            dma((2, n_shot)),
        ],
        compiler_params=pltpu.CompilerParams(
            collective_id=0,
            has_side_effects=True,
            vmem_limit_bytes=52 * 1024 * 1024,
        ),
        name="lsrtm",
    )(
        courant,
        direction,
        back_prev,
        back_now,
        scat_prev,
        scat_now,
        back_end,
        back_before_end,
        back_band,
        absorb,
        wavelet,
        grad_norm,
        src_pos,
        rec_pos,
        residual,
    )
    step_size = scal[0, 0]
    ratio = scal[8, 0]
    return (
        model_image + step_size * direction,
        gradient + ratio * direction,
        residual_new,
    )


def solution(mesh):
    field = P("shot", "gx", None, None)
    grid = P("gx", None, None)
    in_specs = (
        grid,
        P(),
        grid,
        grid,
        field,
        field,
        field,
        field,
        field,
        field,
        P("shot", None, "gx", None, None),
        P("shot", None, None),
        P("shot", None),
        P("shot", "gx", None),
        P("shot", None, "gx"),
        P(),
    )
    return jax.shard_map(
        functools.partial(per_device, mesh.shape["shot"], mesh.shape["gx"]),
        mesh=mesh,
        in_specs=in_specs,
        out_specs=(grid, grid, P("shot", None, "gx")),
        check_vma=False,
    )
```

```python
import functools

import jax
import jax.numpy as jnp
from jax import lax
from jax.experimental import pallas as pl
from jax.experimental.pallas import tpu as pltpu
from jax.sharding import PartitionSpec as P

damp_peak = 0.4
tiny = 1e-6
CX, NY, NZ = 8, 64, 256
NS, STEPS, REC, SRC = 2, 4, 128, 64
PY = 80
HU = 3
CU = CX + 2 * HU
HALF = 128
MESH = pl.DeviceIdType.MESH
f32 = jnp.float32
bf16 = jnp.bfloat16


def split2(v):
    hi = v.astype(bf16)
    lo = (v - hi.astype(f32)).astype(bf16)
    return hi, lo


def profile(pos, extent, low, high):
    gap = extent - 1 - pos
    low_f = low.astype(f32)
    high_f = high.astype(f32)
    near_low = jnp.where(pos < low, ((low - pos).astype(f32) / low_f) ** 2, 0.0)
    near_high = jnp.where(gap < high, ((high - gap).astype(f32) / high_f) ** 2, 0.0)
    return damp_peak * (near_low + near_high)


def kernel(
    n_shot,
    n_gx,
    courant_h,
    direction_h,
    back_prev_h,
    back_now_h,
    scat_prev_h,
    scat_now_h,
    back_end_h,
    back_before_h,
    band_h,
    absorb,
    wavelet,
    grad_norm,
    src_pos,
    rec_pos,
    residual,
    grad_o,
    resid_o,
    scal_o,
    F0,
    F1,
    R0,
    R1,
    U0,
    U1,
    band,
    c0,
    dirv,
    ca,
    cb,
    cc,
    inv,
    cnt,
    rowhot,
    zt,
    zh2,
    info,
    info_n,
    tr,
    tr_n,
    amt_s,
    img_r,
    img_t,
    rs,
    ebuf,
    eslot_s,
    eslot_g,
    ld_sem,
    f_send,
    f_recv,
    r_send,
    r_recv,
    h_send,
    h_recv,
    e_send_s,
    e_recv_s,
    e_send_g,
    e_recv_g,
    g_send,
    g_recv,
):
    me_s = lax.axis_index("shot")
    me_g = lax.axis_index("gx")
    has_left = me_g > 0
    has_right = me_g < n_gx - 1
    F = (F0, F1)
    R = (R0, R1)
    U = (U0, U1)
    own = pl.ds(HU, CX)
    data = pl.ds(8, NY)
    every = slice(None)

    loads = {}
    count_l = [0]

    def load(name, src, dst):
        c = pltpu.make_async_copy(src, dst, ld_sem.at[count_l[0]])
        count_l[0] += 1
        c.start()
        loads.setdefault(name, []).append(c)

    def wait_load(name):
        for c in loads[name]:
            c.wait()

    def load_field(name, src, dst):
        for z in range(2):
            load(name, src.at[:, :, :, pl.ds(z * HALF, HALF)], dst.at[:, z, pl.ds(1, CX), data, :])

    load_field("b0", back_now_h, F0.at[0])
    load_field("s0", scat_now_h, F0.at[1])
    load_field("r0", back_before_h, R0)
    for z in range(2):
        load("c", courant_h.at[:, :, pl.ds(z * HALF, HALF)], c0.at[z, own])
    load_field("bs1", back_prev_h, F1.at[0])
    load_field("bs1", scat_prev_h, F1.at[1])
    for z in range(2):
        load("bs1", direction_h.at[:, :, pl.ds(z * HALF, HALF)], dirv.at[z])
    load_field("r1", back_end_h, R1)
    load("r1", band_h, band)

    zero8 = jnp.zeros((8, HALF), f32)
    zero64 = jnp.zeros((NY, HALF), f32)
    lead_f = [(f, s, z) for f in range(2) for s in range(NS) for z in range(2)]
    lead_r = [(s, z) for s in range(NS) for z in range(2)]
    for p in (0, CX + 1):
        for b in range(2):
            for idx in lead_f:
                F[b][idx + (p, data, every)] = zero64
            for idx in lead_r:
                R[b][idx + (p, data, every)] = zero64
    for z in range(2):
        for p in range(HU):
            c0[z, p] = zero64
            c0[z, HU + CX + p] = zero64
    for g in range(2):
        info_n[g, pl.ds(0, 8), :] = zero8
        info_n[g, pl.ds(8, 8), :] = zero8
        tr_n[g] = zero8

    bar = pltpu.get_barrier_semaphore()
    for d in range(1, n_gx):
        pl.semaphore_signal(
            bar, inc=1, device_id=(me_s, lax.rem(me_g + d, n_gx)), device_id_type=MESH
        )
    for d in range(1, n_shot):
        pl.semaphore_signal(
            bar, inc=1, device_id=(lax.rem(me_s + d, n_shot), me_g), device_id_type=MESH
        )

    rec_row = (rec_pos[0, 0:1, :] * NY + rec_pos[1, 0:1, :]).astype(f32)
    rec_z = rec_pos[2, 0:1, :].astype(f32)
    for s in range(NS):
        info[pl.ds(s * STEPS, STEPS), :] = residual[s]
    info[pl.ds(8, 1), :] = rec_row
    info[pl.ds(9, 1), :] = rec_z
    info[pl.ds(10, 6), :] = jnp.zeros((6, REC), f32)

    class Pair:
        def __init__(self, to_left, to_right, send, recv):
            self.refs = (to_left, to_right)
            self.send = send
            self.recv = recv

        def copy(self, side):
            src, dst = self.refs[side]
            return pltpu.make_async_remote_copy(
                src_ref=src,
                dst_ref=dst,
                send_sem=self.send.at[side],
                recv_sem=self.recv.at[side],
                device_id=(me_s, me_g - 1 if side == 0 else me_g + 1),
                device_id_type=MESH,
            )

        def start(self):
            @pl.when(has_left)
            def _():
                self.copy(0).start()

            @pl.when(has_right)
            def _():
                self.copy(1).start()

        def wait_recv(self):
            @pl.when(has_right)
            def _():
                self.copy(0).wait_recv()

            @pl.when(has_left)
            def _():
                self.copy(1).wait_recv()

        def wait_send(self):
            @pl.when(has_left)
            def _():
                self.copy(0).wait_send()

            @pl.when(has_right)
            def _():
                self.copy(1).wait_send()

    def face(buf, lead, p):
        return buf.at[(every,) * lead + (p, data, every)]

    def bs_faces(n):
        b = F[n % 2]
        return Pair(
            (face(b, 3, 1), face(b, 3, CX + 1)),
            (face(b, 3, CX), face(b, 3, 0)),
            f_send.at[n],
            f_recv.at[n],
        )

    def r_faces(n):
        b = R[n % 2]
        return Pair(
            (face(b, 2, 1), face(b, 2, CX + 1)),
            (face(b, 2, CX), face(b, 2, 0)),
            r_send.at[n],
            r_recv.at[n],
        )

    c_halo = Pair(
        (c0.at[:, pl.ds(HU, HU)], c0.at[:, pl.ds(HU + CX, HU)]),
        (c0.at[:, pl.ds(CX, HU)], c0.at[:, pl.ds(0, HU)]),
        h_send.at[0],
        h_recv.at[0],
    )
    info_halo = Pair((info, info_n.at[1]), (info, info_n.at[0]), h_send.at[1], h_recv.at[1])
    tr_halo = Pair((tr, tr_n.at[1]), (tr, tr_n.at[0]), h_send.at[2], h_recv.at[2])

    pl.semaphore_wait(bar, n_gx - 1 + n_shot - 1)
    wait_load("b0")
    wait_load("s0")
    bs_faces(0).start()
    wait_load("r0")
    r_faces(0).start()
    info_halo.start()
    wait_load("c")
    c_halo.start()

    def pads(p, carry):
        for b in range(2):
            for idx in lead_f:
                F[b][idx + (p, pl.ds(0, 8), every)] = zero8
                F[b][idx + (p, pl.ds(72, 8), every)] = zero8
            for idx in lead_r:
                R[b][idx + (p, pl.ds(0, 8), every)] = zero8
                R[b][idx + (p, pl.ds(72, 8), every)] = zero8
        return carry

    lax.fori_loop(0, CX + 2, pads, 0)

    def pads_u(p, carry):
        for b in range(2):
            for idx in lead_r:
                U[b][idx + (p, pl.ds(0, 8), every)] = zero8
                U[b][idx + (p, pl.ds(72, 8), every)] = zero8
        return carry

    lax.fori_loop(0, CU, pads_u, 0)

    def to_col(row, n):
        eye = lax.broadcasted_iota(jnp.int32, (n, n), 0) == lax.broadcasted_iota(
            jnp.int32, (n, n), 1
        )
        return jnp.sum(jnp.where(eye, row, 0.0), axis=1, keepdims=True)

    first_row = ((me_g * CX - HU) * NY).astype(f32)

    def hot_rows(row, lo, n):
        rows = lax.broadcasted_iota(jnp.int32, (n, REC), 0).astype(f32) + (first_row + lo)
        rowhot[pl.ds(lo, n), :] = jnp.where(rows == row, 1.0, 0.0).astype(bf16)

    lane_z = lax.broadcasted_iota(jnp.int32, (REC, NZ), 1).astype(f32)

    def hot_z(z_row, g):
        hot = jnp.where(lane_z == to_col(z_row, REC), 1.0, 0.0).astype(bf16)
        zh2[g, pl.ds(0, REC), :] = hot
        zh2[g, pl.ds(REC, REC), :] = hot

    hot_rows(rec_row, HU * NY, CX * NY)
    hot_z(rec_z, 1)
    zt[...] = jnp.where(
        lax.broadcasted_iota(jnp.int32, (NZ, REC), 0).astype(f32) == rec_z, 1.0, 0.0
    ).astype(bf16)

    nx = n_gx * CX
    lane = lax.broadcasted_iota(jnp.int32, (8, HALF), 1)
    sub = lax.broadcasted_iota(jnp.int32, (8, HALF), 0)
    damp_z = [profile(lane + z * HALF, NZ, absorb[4], absorb[5]) for z in range(2)]

    def coef(i, carry):
        pos_x = jnp.full((8, HALF), me_g * CX - HU + i, jnp.int32)
        damp_x = profile(pos_x, nx, absorb[0], absorb[1])
        for y in range(8):
            ys = pl.ds(y * 8, 8)
            damp_xy = damp_x + profile(sub + y * 8, NY, absorb[2], absorb[3])
            for z in range(2):
                damping = damp_xy + damp_z[z]
                c = c0[z, i, ys, :]
                iv = 1.0 / (1.0 + damping)
                inv[z, i, ys, :] = iv
                ca[z, i, ys, :] = (2.0 - 6.0 * c) * iv
                cb[z, i, ys, :] = (1.0 - damping) * iv
                cc[z, i, ys, :] = c * iv
        return carry

    lax.fori_loop(HU, HU + CX, coef, 0)

    src_hot = []
    for s in range(NS):
        s_row = ((src_pos[0, s : s + 1, :] - me_g * CX) * NY + src_pos[1, s : s + 1, :]).astype(
            f32
        )
        s_z = to_col(src_pos[2, s : s + 1, :].astype(f32), SRC)
        s_hot = jnp.where(
            lax.broadcasted_iota(jnp.int32, (SRC, NZ), 1).astype(f32) == s_z, 1.0, 0.0
        ).astype(bf16)
        src_hot.append((s_row, s_hot))

    def count(p, carry):
        rows = (lax.broadcasted_iota(jnp.int32, (NY, SRC), 0) + p * NY).astype(f32)
        for s in range(NS):
            hot = jnp.where(rows == src_hot[s][0], 1.0, 0.0).astype(bf16)
            n = jnp.dot(hot, src_hot[s][1], preferred_element_type=f32)
            for z in range(2):
                cnt[s, z, p] = n[:, z * HALF : (z + 1) * HALF] * inv[z, HU + p]
        return carry

    lax.fori_loop(0, CX, count, 0, unroll=2)

    first = lane == 0
    last = lane == HALF - 1

    def neighbours(ref, lead, p, y8):
        ys = pl.ds(8 + y8, 8)
        mid = [ref[lead + (z, p, ys, every)] for z in range(2)]
        right = [pltpu.roll(m, 1, 1) for m in mid]
        left = [pltpu.roll(m, HALF - 1, 1) for m in mid]
        low = [jnp.where(first, 0.0, right[0]), jnp.where(first, right[0], right[1])]
        high = [jnp.where(last, left[1], left[0]), jnp.where(last, 0.0, left[1])]
        sums = []
        for z in range(2):
            t = ref[lead + (z, p + 1, ys, every)] + ref[lead + (z, p - 1, ys, every)]
            t = t + (
                ref[lead + (z, p, pl.ds(y8 + 9, 8), every)]
                + ref[lead + (z, p, pl.ds(y8 + 7, 8), every)]
            )
            sums.append(t + (low[z] + high[z]))
        return mid, sums

    def step_bs(n, p):
        now, nxt = F[n % 2], F[(n + 1) % 2]
        q = p - 1
        i = q + HU

        def chunk(j, carry):
            y8 = pl.multiple_of(j * 8, 8)
            ys = pl.ds(y8, 8)
            ysp = pl.ds(pl.multiple_of(y8 + 8, 8), 8)
            a = [ca[z, i, ys, :] for z in range(2)]
            b = [cb[z, i, ys, :] for z in range(2)]
            c = [cc[z, i, ys, :] for z in range(2)]
            di = [dirv[z, q, ys, :] for z in range(2)]
            for s in range(NS):
                w = wavelet[s, n]
                mid, sums = neighbours(now, (0, s), p, y8)
                acc = []
                for z in range(2):
                    old = nxt[0, s, z, p, ysp, :]
                    new = (
                        a[z] * mid[z]
                        - b[z] * old
                        + c[z] * sums[z]
                        + w * cnt[s, z, q, ys, :]
                    )
                    nxt[0, s, z, p, ysp, :] = new
                    acc.append((new - mid[z]) - (mid[z] - old))
                mid, sums = neighbours(now, (1, s), p, y8)
                for z in range(2):
                    old = nxt[1, s, z, p, ysp, :]
                    nxt[1, s, z, p, ysp, :] = (
                        a[z] * mid[z] - b[z] * old + c[z] * (sums[z] - di[z] * acc[z])
                    )
            return carry

        lax.fori_loop(0, 8, chunk, 0, unroll=8)

    def step_r(n, p):
        now, nxt = R[n % 2], R[(n + 1) % 2]
        q = p - 1
        i = q + HU
        m = STEPS - 1 - n

        def chunk(j, carry):
            y8 = pl.multiple_of(j * 8, 8)
            ys = pl.ds(y8, 8)
            ysp = pl.ds(pl.multiple_of(y8 + 8, 8), 8)
            a = [ca[z, i, ys, :] for z in range(2)]
            c = [cc[z, i, ys, :] for z in range(2)]
            layer = [cb[z, i, ys, :] < 1.0 for z in range(2)]
            for s in range(NS):
                w = wavelet[s, m]
                mid, sums = neighbours(now, (s,), p, y8)
                for z in range(2):
                    zs = pl.ds(z * HALF, HALF)
                    old = nxt[s, z, p, ysp, :]
                    new = a[z] * mid[z] - old + c[z] * sums[z] + w * cnt[s, z, q, ys, :]
                    new = jnp.where(layer[z], band[s, m, q, ys, zs], new)
                    nxt[s, z, p, ysp, :] = new
                    band[s, m, q, ys, zs] = (new - mid[z]) - (mid[z] - old)
            return carry

        lax.fori_loop(0, 8, chunk, 0, unroll=8)

    def gather(n):
        ref = F[(n + 1) % 2]
        zero = jnp.zeros((NY, REC), f32)

        def one(p, carry):
            hot = rowhot[pl.ds(pl.multiple_of((p + HU) * NY, NY), NY), :].astype(f32)
            parts = []
            for s in range(NS):
                v = jnp.concatenate([ref[1, s, z, p + 1, data, :] for z in range(2)], axis=1)
                parts.extend(split2(v))
            g = jnp.dot(jnp.concatenate(parts, axis=0), zt[...], preferred_element_type=f32)
            return tuple(
                carry[s] + hot * (g[2 * s * NY : (2 * s + 1) * NY] + g[(2 * s + 1) * NY : (2 * s + 2) * NY])
                for s in range(NS)
            )

        got = lax.fori_loop(0, CX, one, (zero, zero), unroll=4)
        for s in range(NS):
            tr[pl.ds(s * STEPS + n, 1), :] = jnp.sum(got[s], axis=0, keepdims=True)

    def inject(m, amounts, lo, hi):
        nxt = U[m % 2]
        n = STEPS - 1 - m

        def plane(i, carry):
            g = (i + CX - HU) // CX
            hot = rowhot[pl.ds(pl.multiple_of(i * NY, NY), NY), :].astype(f32)
            parts = []
            for s in range(NS):
                v = amounts[g, pl.ds(s * STEPS + n, 1), :]
                v_hi = v.astype(bf16).astype(f32)
                parts.append(
                    jnp.concatenate(
                        [(hot * v_hi).astype(bf16), (hot * (v - v_hi)).astype(bf16)], axis=1
                    )
                )
            e = jnp.dot(jnp.concatenate(parts, axis=0), zh2[g], preferred_element_type=f32)
            for s in range(NS):
                for z in range(2):
                    u = inv[z, i] * e[s * NY : (s + 1) * NY, z * HALF : (z + 1) * HALF]
                    if m > 1:
                        u = u - cb[z, i] * nxt[s, z, i, data, :]
                    nxt[s, z, i, data, :] = u
            return carry

        lax.fori_loop(lo, hi, plane, 0, unroll=2)

    def level(m, img):
        now, nxt = U[(m + 1) % 2], U[m % 2]
        n = STEPS - 1 - m

        def plane(image, i, carry):
            q = i - HU

            def chunk(j, inner):
                y8 = pl.multiple_of(j * 8, 8)
                ys = pl.ds(y8, 8)
                ysp = pl.ds(pl.multiple_of(y8 + 8, 8), 8)
                pic = [None, None]
                for s in range(NS):
                    if m > 0:
                        mid, sums = neighbours(now, (s,), i, y8)
                    for z in range(2):
                        u = nxt[s, z, i, ysp, :]
                        if m > 0:
                            u = u + ca[z, i, ys, :] * mid[z] + cc[z, i, ys, :] * sums[z]
                            if m < STEPS - 1:
                                nxt[s, z, i, ysp, :] = u
                        if image:
                            part = band[s, n, q, ys, pl.ds(z * HALF, HALF)] * u
                            pic[z] = part if s == 0 else pic[z] + part
                if image:
                    for z in range(2):
                        zs = pl.ds(z * HALF, HALF)
                        old = 0.0 if m == 0 else img[q, ys, zs]
                        img[q, ys, zs] = old + pic[z]
                return inner

            lax.fori_loop(0, 8, chunk, 0, unroll=8)
            return carry

        if 0 < m < STEPS - 1:
            lax.fori_loop(m, HU, functools.partial(plane, False), 0)
            lax.fori_loop(HU + CX, CU - m, functools.partial(plane, False), 0)
        lax.fori_loop(HU, HU + CX, functools.partial(plane, True), 0)

    for n in range(STEPS):
        bs_faces(n).wait_recv()
        if n == 0:
            wait_load("bs1")
        if n > 0:
            bs_faces(n - 1).wait_send()

        def edge_bs(k, carry):
            step_bs(n, 1 + (CX - 1) * k)
            return carry

        lax.fori_loop(0, 2, edge_bs, 0)
        if n < STEPS - 1:
            bs_faces(n + 1).start()
        r_faces(n).wait_recv()
        if n == 0:
            wait_load("r1")
        if n > 0:
            r_faces(n - 1).wait_send()

        def edge_r(k, carry):
            step_r(n, 1 + (CX - 1) * k)
            return carry

        lax.fori_loop(0, 2, edge_r, 0)
        if n < STEPS - 1:
            r_faces(n + 1).start()

        def inner_bs(p, carry):
            step_bs(n, p)
            return carry

        lax.fori_loop(2, CX, inner_bs, 0)

        def inner_r(p, carry):
            step_r(n, p)
            return carry

        lax.fori_loop(2, CX, inner_r, 0)
        gather(n)
        if n == 0:
            info_halo.wait_recv()
            c_halo.wait_recv()
            for g, lo in ((0, 0), (1, (HU + CX) * NY)):
                hot_rows(info_n[g, pl.ds(8, 1), :], lo, HU * NY)
                hot_z(info_n[g, pl.ds(9, 1), :], 2 * g)
            lax.fori_loop(0, HU, coef, 0)
            lax.fori_loop(HU + CX, CU, coef, 0)
            amt_s[0, 0] = info_n[0, pl.ds(0, 8), :]
            amt_s[0, 1] = info[pl.ds(0, 8), :]
            amt_s[0, 2] = info_n[1, pl.ds(0, 8), :]
        inject(n, amt_s.at[0], n, CU - n)
        level(n, img_r)
    bs_faces(STEPS - 1).wait_send()
    r_faces(STEPS - 1).wait_send()
    info_halo.wait_send()
    c_halo.wait_send()

    def to_shots(r):
        return [
            pltpu.make_async_remote_copy(
                src_ref=ebuf.at[r, 0],
                dst_ref=eslot_s.at[r, me_s],
                send_sem=e_send_s.at[r, d],
                recv_sem=e_recv_s.at[r, d],
                device_id=(lax.rem(me_s + d, n_shot), me_g),
                device_id_type=MESH,
            )
            for d in range(1, n_shot)
        ]

    def to_slabs(r):
        return [
            pltpu.make_async_remote_copy(
                src_ref=ebuf.at[r, 1],
                dst_ref=eslot_g.at[r, me_g],
                send_sem=e_send_g.at[r, d],
                recv_sem=e_recv_g.at[r, d],
                device_id=(me_s, lax.rem(me_g + d, n_gx)),
                device_id_type=MESH,
            )
            for d in range(1, n_gx)
        ]

    def sum_start(value, r):
        ebuf[r, 0] = value
        eslot_s[r, me_s] = value
        for c in to_shots(r):
            c.start()

    def sum_middle(r):
        for c in to_shots(r):
            c.wait_recv()
        total = eslot_s[r, 0]
        for d in range(1, n_shot):
            total = total + eslot_s[r, d]
        ebuf[r, 1] = total
        eslot_g[r, me_g] = total
        for c in to_slabs(r):
            c.start()

    def sum_end(r):
        for c in to_slabs(r):
            c.wait_recv()
        total = eslot_g[r, 0]
        for d in range(1, n_gx):
            total = total + eslot_g[r, d]
        return jnp.sum(total)

    t = tr[...]
    tr_halo.start()
    sum_start(t * t, 0)
    amt_s[1, 1] = t
    inject(0, amt_s.at[1], HU, HU + CX)
    tr_halo.wait_recv()
    amt_s[1, 0] = tr_n[0]
    amt_s[1, 2] = tr_n[1]
    inject(0, amt_s.at[1], 0, HU)
    inject(0, amt_s.at[1], HU + CX, CU)
    level(0, img_t)
    sum_middle(0)
    for m in range(1, STEPS):
        inject(m, amt_s.at[1], m, CU - m)
        level(m, img_t)
    energy = sum_end(0)
    gn = jnp.full((8, HALF), grad_norm[0], f32)
    step = gn / (jnp.full((8, HALF), energy, f32) + tiny)
    for s in range(NS):
        resid_o[s] = residual[s] - step[0:STEPS] * t[s * STEPS : (s + 1) * STEPS]

    def combine(q):
        for y in range(8):
            ys = pl.ds(y * 8, 8)
            for z in range(2):
                zs = pl.ds(z * HALF, HALF)
                img_r[q, ys, zs] = c0[z, HU + q, ys, :] * (
                    step * img_t[q, ys, zs] - img_r[q, ys, zs]
                )

    scatter = []
    for d in range(1, n_shot):
        to = lax.rem(me_s + d, n_shot)
        combine(to)
        c = pltpu.make_async_remote_copy(
            src_ref=img_r.at[to],
            dst_ref=rs.at[d - 1],
            send_sem=g_send.at[0, d],
            recv_sem=g_recv.at[0, d],
            device_id=(to, me_g),
            device_id_type=MESH,
        )
        c.start()
        scatter.append(c)
    combine(me_s)
    for c in scatter:
        c.wait_recv()

    def add(i, carry):
        ys = pl.ds(pl.multiple_of(i * 8, 8), 8)
        g = img_r[me_s, ys, :]
        for d in range(1, n_shot):
            g = g + rs[d - 1, ys, :]
        grad_o[me_s, ys, :] = g
        g = g * g
        return carry + (g[:, :HALF] + g[:, HALF:])

    part = lax.fori_loop(0, 8, add, jnp.zeros((8, HALF), f32), unroll=8)
    sum_start(part, 1)
    spread = []
    for d in range(1, n_shot):
        to = lax.rem(me_s + d, n_shot)
        c = pltpu.make_async_remote_copy(
            src_ref=grad_o.at[me_s],
            dst_ref=grad_o.at[me_s],
            send_sem=g_send.at[1, d],
            recv_sem=g_recv.at[1, d],
            device_id=(to, me_g),
            device_id_type=MESH,
        )
        c.start()
        spread.append(c)
    sum_middle(1)
    grad_energy = sum_end(1)
    ratio = jnp.full((8, HALF), grad_energy, f32) / gn
    scal_o[pl.ds(0, 8), :] = step
    scal_o[pl.ds(8, 8), :] = ratio
    for d in range(1, n_shot):
        came = lax.rem(me_s + n_shot - d, n_shot)
        pltpu.make_async_remote_copy(
            src_ref=grad_o.at[came],
            dst_ref=grad_o.at[came],
            send_sem=g_send.at[1, d],
            recv_sem=g_recv.at[1, d],
            device_id=(came, me_g),
            device_id_type=MESH,
        ).wait_recv()
    tr_halo.wait_send()
    for r in range(2):
        for c in to_shots(r) + to_slabs(r):
            c.wait_send()
    for c in scatter + spread:
        c.wait_send()


def finish(scal, gradient, direction, model_image, resid, image_o, dir_o, resid_o):
    step = scal[0:1, 0:1]
    ratio = scal[8:9, 0:1]

    def plane(p, carry):
        d = direction[p]
        image_o[p] = model_image[p] + step * d
        dir_o[p] = gradient[p] + ratio * d
        return carry

    lax.fori_loop(0, CX, plane, 0)
    resid_o[...] = resid[...]


def per_device(
    n_shot,
    n_gx,
    courant,
    absorb,
    model_image,
    direction,
    back_prev,
    back_now,
    scat_prev,
    scat_now,
    back_end,
    back_before_end,
    back_band,
    src_pos,
    wavelet,
    rec_pos,
    residual,
    grad_norm,
):
    hbm = pl.BlockSpec(memory_space=pl.ANY)
    vmem = pl.BlockSpec(memory_space=pltpu.VMEM)
    smem = pl.BlockSpec(memory_space=pltpu.SMEM)
    slab = (2, CX, NY, HALF)
    wide = (2, CU, NY, HALF)
    dma = pltpu.SemaphoreType.DMA
    V = pltpu.VMEM
    gradient, resid, scal = pl.pallas_call(
        functools.partial(kernel, n_shot, n_gx),
        out_shape=(
            jax.ShapeDtypeStruct((CX, NY, NZ), f32),
            jax.ShapeDtypeStruct((NS, STEPS, REC), f32),
            jax.ShapeDtypeStruct((16, HALF), f32),
        ),
        in_specs=[hbm] * 9 + [smem] * 3 + [vmem] * 3,
        out_specs=(vmem, vmem, vmem),
        scratch_shapes=[
            V((2, NS, 2, CX + 2, PY, HALF), f32),
            V((2, NS, 2, CX + 2, PY, HALF), f32),
            V((NS, 2, CX + 2, PY, HALF), f32),
            V((NS, 2, CX + 2, PY, HALF), f32),
            V((NS, 2, CU, PY, HALF), f32),
            V((NS, 2, CU, PY, HALF), f32),
            V((NS, STEPS, CX, NY, NZ), f32),
            V(wide, f32),
            V(slab, f32),
            V(wide, f32),
            V(wide, f32),
            V(wide, f32),
            V(wide, f32),
            V((NS,) + slab, f32),
            V((CU * NY, REC), bf16),
            V((NZ, REC), bf16),
            V((3, 2 * REC, NZ), bf16),
            V((16, REC), f32),
            V((2, 16, REC), f32),
            V((NS * STEPS, REC), f32),
            V((2, NS * STEPS, REC), f32),
            V((2, 3, NS * STEPS, REC), f32),
            V((CX, NY, NZ), f32),
            V((CX, NY, NZ), f32),
            V((n_shot - 1, NY, NZ), f32),
            V((2, 2, 8, HALF), f32),
            V((2, n_shot, 8, HALF), f32),
            V((2, n_gx, 8, HALF), f32),
            dma((17,)),
            dma((STEPS, 2)),
            dma((STEPS, 2)),
            dma((STEPS, 2)),
            dma((STEPS, 2)),
            dma((3, 2)),
            dma((3, 2)),
            dma((2, n_shot)),
            dma((2, n_shot)),
            dma((2, n_gx)),
            dma((2, n_gx)),
            dma((2, n_shot)),
            dma((2, n_shot)),
        ],
        compiler_params=pltpu.CompilerParams(
            collective_id=0,
            has_side_effects=True,
            vmem_limit_bytes=58 * 1024 * 1024,
        ),
        name="lsrtm",
    )(
        courant,
        direction,
        back_prev,
        back_now,
        scat_prev,
        scat_now,
        back_end,
        back_before_end,
        back_band,
        absorb,
        wavelet,
        grad_norm,
        jnp.transpose(src_pos, (2, 0, 1)),
        jnp.transpose(rec_pos, (2, 0, 1)),
        residual,
    )
    return pl.pallas_call(
        finish,
        out_shape=(
            jax.ShapeDtypeStruct((CX, NY, NZ), f32),
            jax.ShapeDtypeStruct((CX, NY, NZ), f32),
            jax.ShapeDtypeStruct((NS, STEPS, REC), f32),
        ),
        in_specs=[vmem] * 5,
        out_specs=(vmem, vmem, vmem),
        compiler_params=pltpu.CompilerParams(vmem_limit_bytes=16 * 1024 * 1024),
        name="finish",
    )(scal, gradient, direction, model_image, resid)


def solution(mesh):
    field = P("shot", "gx", None, None)
    grid = P("gx", None, None)
    in_specs = (
        grid,
        P(),
        grid,
        grid,
        field,
        field,
        field,
        field,
        field,
        field,
        P("shot", None, "gx", None, None),
        P("shot", None, None),
        P("shot", None),
        P("shot", "gx", None),
        P("shot", None, "gx"),
        P(),
    )
    return jax.shard_map(
        functools.partial(per_device, mesh.shape["shot"], mesh.shape["gx"]),
        mesh=mesh,
        in_specs=in_specs,
        out_specs=(grid, grid, P("shot", None, "gx")),
        check_vma=False,
    )
```

```python
import functools

import jax
import jax.numpy as jnp
from jax import lax
from jax.experimental import pallas as pl
from jax.experimental.pallas import tpu as pltpu
from jax.sharding import PartitionSpec as P

damp_peak = 0.4
tiny = 1e-6
CX, NY, NZ = 8, 64, 256
NS, STEPS, REC, SRC = 2, 4, 128, 64
PY = 80
HU = 3
CU = CX + 2 * HU
HALF = 128
MESH = pl.DeviceIdType.MESH
f32 = jnp.float32
bf16 = jnp.bfloat16


def split2(v):
    hi = v.astype(bf16)
    lo = (v - hi.astype(f32)).astype(bf16)
    return hi, lo


def profile(pos, extent, low, high):
    gap = extent - 1 - pos
    low_f = low.astype(f32)
    high_f = high.astype(f32)
    near_low = jnp.where(pos < low, ((low - pos).astype(f32) / low_f) ** 2, 0.0)
    near_high = jnp.where(gap < high, ((high - gap).astype(f32) / high_f) ** 2, 0.0)
    return damp_peak * (near_low + near_high)


def kernel(
    n_shot,
    n_gx,
    courant_h,
    direction_h,
    back_prev_h,
    back_now_h,
    scat_prev_h,
    scat_now_h,
    back_end_h,
    back_before_h,
    band_h,
    absorb,
    wavelet,
    grad_norm,
    src_pos,
    rec_pos,
    residual,
    grad_o,
    resid_o,
    scal_o,
    F0,
    F1,
    R0,
    R1,
    U0,
    U1,
    band,
    c0,
    dirv,
    ca,
    cb,
    cc,
    inv,
    cnt,
    rowhot,
    zt,
    zh2,
    info,
    info_n,
    tr,
    tr_n,
    amt_s,
    E,
    img_r,
    img_t,
    rs,
    ebuf,
    eslot_s,
    eslot_g,
    ld_sem,
    f_send,
    f_recv,
    r_send,
    r_recv,
    h_send,
    h_recv,
    e_send_s,
    e_recv_s,
    e_send_g,
    e_recv_g,
    g_send,
    g_recv,
):
    me_s = lax.axis_index("shot")
    me_g = lax.axis_index("gx")
    has_left = me_g > 0
    has_right = me_g < n_gx - 1
    F = (F0, F1)
    R = (R0, R1)
    U = (U0, U1)
    own = pl.ds(HU, CX)
    data = pl.ds(8, NY)
    every = slice(None)

    loads = {}
    count_l = [0]

    def load(name, src, dst):
        c = pltpu.make_async_copy(src, dst, ld_sem.at[count_l[0]])
        count_l[0] += 1
        c.start()
        loads.setdefault(name, []).append(c)

    def wait_load(name):
        for c in loads[name]:
            c.wait()

    def load_field(name, src, dst):
        for z in range(2):
            load(name, src.at[:, :, :, pl.ds(z * HALF, HALF)], dst.at[:, z, pl.ds(1, CX), data, :])

    load_field("b0", back_now_h, F0.at[0])
    load_field("s0", scat_now_h, F0.at[1])
    load_field("r0", back_before_h, R0)
    for z in range(2):
        load("c", courant_h.at[:, :, pl.ds(z * HALF, HALF)], c0.at[z, own])
    load_field("bs1", back_prev_h, F1.at[0])
    load_field("bs1", scat_prev_h, F1.at[1])
    for z in range(2):
        load("bs1", direction_h.at[:, :, pl.ds(z * HALF, HALF)], dirv.at[z])
    load_field("r1", back_end_h, R1)
    load("r1", band_h, band)

    zero8 = jnp.zeros((8, HALF), f32)
    zero64 = jnp.zeros((NY, HALF), f32)
    lead_f = [(f, s, z) for f in range(2) for s in range(NS) for z in range(2)]
    lead_r = [(s, z) for s in range(NS) for z in range(2)]
    for p in (0, CX + 1):
        for b in range(2):
            for idx in lead_f:
                F[b][idx + (p, data, every)] = zero64
            for idx in lead_r:
                R[b][idx + (p, data, every)] = zero64
    for z in range(2):
        for p in range(HU):
            c0[z, p] = zero64
            c0[z, HU + CX + p] = zero64
    for g in range(2):
        info_n[g, pl.ds(0, 8), :] = zero8
        info_n[g, pl.ds(8, 8), :] = zero8
        tr_n[g] = zero8

    bar = pltpu.get_barrier_semaphore()
    for d in range(1, n_gx):
        pl.semaphore_signal(
            bar, inc=1, device_id=(me_s, lax.rem(me_g + d, n_gx)), device_id_type=MESH
        )
    for d in range(1, n_shot):
        pl.semaphore_signal(
            bar, inc=1, device_id=(lax.rem(me_s + d, n_shot), me_g), device_id_type=MESH
        )

    rec_row = (rec_pos[0, 0:1, :] * NY + rec_pos[1, 0:1, :]).astype(f32)
    rec_z = rec_pos[2, 0:1, :].astype(f32)
    for s in range(NS):
        info[pl.ds(s * STEPS, STEPS), :] = residual[s]
    info[pl.ds(8, 1), :] = rec_row
    info[pl.ds(9, 1), :] = rec_z
    info[pl.ds(10, 6), :] = jnp.zeros((6, REC), f32)

    class Pair:
        def __init__(self, to_left, to_right, send, recv):
            self.refs = (to_left, to_right)
            self.send = send
            self.recv = recv

        def copy(self, side):
            src, dst = self.refs[side]
            return pltpu.make_async_remote_copy(
                src_ref=src,
                dst_ref=dst,
                send_sem=self.send.at[side],
                recv_sem=self.recv.at[side],
                device_id=(me_s, me_g - 1 if side == 0 else me_g + 1),
                device_id_type=MESH,
            )

        def start(self):
            @pl.when(has_left)
            def _():
                self.copy(0).start()

            @pl.when(has_right)
            def _():
                self.copy(1).start()

        def wait_recv(self):
            @pl.when(has_right)
            def _():
                self.copy(0).wait_recv()

            @pl.when(has_left)
            def _():
                self.copy(1).wait_recv()

        def wait_send(self):
            @pl.when(has_left)
            def _():
                self.copy(0).wait_send()

            @pl.when(has_right)
            def _():
                self.copy(1).wait_send()

    def face(buf, lead, p):
        return buf.at[(every,) * lead + (p, data, every)]

    def bs_faces(n):
        b = F[n % 2]
        return Pair(
            (face(b, 3, 1), face(b, 3, CX + 1)),
            (face(b, 3, CX), face(b, 3, 0)),
            f_send.at[n],
            f_recv.at[n],
        )

    def r_faces(n):
        b = R[n % 2]
        return Pair(
            (face(b, 2, 1), face(b, 2, CX + 1)),
            (face(b, 2, CX), face(b, 2, 0)),
            r_send.at[n],
            r_recv.at[n],
        )

    c_halo = Pair(
        (c0.at[:, pl.ds(HU, HU)], c0.at[:, pl.ds(HU + CX, HU)]),
        (c0.at[:, pl.ds(CX, HU)], c0.at[:, pl.ds(0, HU)]),
        h_send.at[0],
        h_recv.at[0],
    )
    info_halo = Pair((info, info_n.at[1]), (info, info_n.at[0]), h_send.at[1], h_recv.at[1])
    tr_halo = Pair((tr, tr_n.at[1]), (tr, tr_n.at[0]), h_send.at[2], h_recv.at[2])

    def pads(p, carry):
        for b in range(2):
            for idx in lead_f:
                F[b][idx + (p, pl.ds(0, 8), every)] = zero8
                F[b][idx + (p, pl.ds(72, 8), every)] = zero8
            for idx in lead_r:
                R[b][idx + (p, pl.ds(0, 8), every)] = zero8
                R[b][idx + (p, pl.ds(72, 8), every)] = zero8
        return carry

    lax.fori_loop(0, CX + 2, pads, 0)

    def pads_u(p, carry):
        for b in range(2):
            for idx in lead_r:
                U[b][idx + (p, pl.ds(0, 8), every)] = zero8
                U[b][idx + (p, pl.ds(72, 8), every)] = zero8
        return carry

    lax.fori_loop(0, CU, pads_u, 0)

    def to_col(row, n):
        eye = lax.broadcasted_iota(jnp.int32, (n, n), 0) == lax.broadcasted_iota(
            jnp.int32, (n, n), 1
        )
        return jnp.sum(jnp.where(eye, row, 0.0), axis=1, keepdims=True)

    first_row = ((me_g * CX - HU) * NY).astype(f32)

    def hot_rows(row, lo, n):
        rows = lax.broadcasted_iota(jnp.int32, (n, REC), 0).astype(f32) + (first_row + lo)
        rowhot[pl.ds(lo, n), :] = jnp.where(rows == row, 1.0, 0.0).astype(bf16)

    lane_z = lax.broadcasted_iota(jnp.int32, (REC, NZ), 1).astype(f32)

    def hot_z(z_row, g):
        hot = jnp.where(lane_z == to_col(z_row, REC), 1.0, 0.0).astype(bf16)
        zh2[g, pl.ds(0, REC), :] = hot
        zh2[g, pl.ds(REC, REC), :] = hot

    hot_rows(rec_row, HU * NY, CX * NY)
    hot_z(rec_z, 1)
    zt[...] = jnp.where(
        lax.broadcasted_iota(jnp.int32, (NZ, REC), 0).astype(f32) == rec_z, 1.0, 0.0
    ).astype(bf16)

    pl.semaphore_wait(bar, n_gx - 1 + n_shot - 1)
    wait_load("b0")
    wait_load("s0")
    bs_faces(0).start()
    wait_load("r0")
    r_faces(0).start()
    info_halo.start()
    wait_load("c")
    c_halo.start()

    nx = n_gx * CX
    lane = lax.broadcasted_iota(jnp.int32, (8, HALF), 1)
    sub = lax.broadcasted_iota(jnp.int32, (8, HALF), 0)
    damp_z = [profile(lane + z * HALF, NZ, absorb[4], absorb[5]) for z in range(2)]

    def coef(i, carry):
        pos_x = jnp.full((8, HALF), me_g * CX - HU + i, jnp.int32)
        damp_x = profile(pos_x, nx, absorb[0], absorb[1])
        for y in range(8):
            ys = pl.ds(y * 8, 8)
            damp_xy = damp_x + profile(sub + y * 8, NY, absorb[2], absorb[3])
            for z in range(2):
                damping = damp_xy + damp_z[z]
                c = c0[z, i, ys, :]
                iv = 1.0 / (1.0 + damping)
                inv[z, i, ys, :] = iv
                ca[z, i, ys, :] = (2.0 - 6.0 * c) * iv
                cb[z, i, ys, :] = (1.0 - damping) * iv
                cc[z, i, ys, :] = c * iv
        return carry

    lax.fori_loop(HU, HU + CX, coef, 0)

    src_hot = []
    for s in range(NS):
        s_row = ((src_pos[0, s : s + 1, :] - me_g * CX) * NY + src_pos[1, s : s + 1, :]).astype(
            f32
        )
        s_z = to_col(src_pos[2, s : s + 1, :].astype(f32), SRC)
        s_hot = jnp.where(
            lax.broadcasted_iota(jnp.int32, (SRC, NZ), 1).astype(f32) == s_z, 1.0, 0.0
        ).astype(bf16)
        src_hot.append((s_row, s_hot))

    def count(p, carry):
        rows = (lax.broadcasted_iota(jnp.int32, (NY, SRC), 0) + p * NY).astype(f32)
        for s in range(NS):
            hot = jnp.where(rows == src_hot[s][0], 1.0, 0.0).astype(bf16)
            n = jnp.dot(hot, src_hot[s][1], preferred_element_type=f32)
            for z in range(2):
                cnt[s, z, p] = n[:, z * HALF : (z + 1) * HALF] * inv[z, HU + p]
        return carry

    lax.fori_loop(0, CX, count, 0, unroll=2)

    first = lane == 0
    last = lane == HALF - 1

    def neighbours(ref, lead, p, y8):
        ys = pl.ds(8 + y8, 8)
        mid = [ref[lead + (z, p, ys, every)] for z in range(2)]
        right = [pltpu.roll(m, 1, 1) for m in mid]
        left = [pltpu.roll(m, HALF - 1, 1) for m in mid]
        low = [jnp.where(first, 0.0, right[0]), jnp.where(first, right[0], right[1])]
        high = [jnp.where(last, left[1], left[0]), jnp.where(last, 0.0, left[1])]
        sums = []
        for z in range(2):
            t = ref[lead + (z, p + 1, ys, every)] + ref[lead + (z, p - 1, ys, every)]
            t = t + (
                ref[lead + (z, p, pl.ds(y8 + 9, 8), every)]
                + ref[lead + (z, p, pl.ds(y8 + 7, 8), every)]
            )
            sums.append(t + (low[z] + high[z]))
        return mid, sums

    def step_bs(n, p):
        now, nxt = F[n % 2], F[(n + 1) % 2]
        q = p - 1
        i = q + HU

        def chunk(j, carry):
            y8 = pl.multiple_of(j * 8, 8)
            ys = pl.ds(y8, 8)
            ysp = pl.ds(pl.multiple_of(y8 + 8, 8), 8)
            a = [ca[z, i, ys, :] for z in range(2)]
            b = [cb[z, i, ys, :] for z in range(2)]
            c = [cc[z, i, ys, :] for z in range(2)]
            di = [dirv[z, q, ys, :] for z in range(2)]
            for s in range(NS):
                w = wavelet[s, n]
                mid, sums = neighbours(now, (0, s), p, y8)
                acc = []
                for z in range(2):
                    old = nxt[0, s, z, p, ysp, :]
                    new = (
                        a[z] * mid[z]
                        - b[z] * old
                        + c[z] * sums[z]
                        + w * cnt[s, z, q, ys, :]
                    )
                    nxt[0, s, z, p, ysp, :] = new
                    acc.append((new - mid[z]) - (mid[z] - old))
                mid, sums = neighbours(now, (1, s), p, y8)
                for z in range(2):
                    old = nxt[1, s, z, p, ysp, :]
                    nxt[1, s, z, p, ysp, :] = (
                        a[z] * mid[z] - b[z] * old + c[z] * (sums[z] - di[z] * acc[z])
                    )
            return carry

        lax.fori_loop(0, 8, chunk, 0, unroll=8)

    def step_r(n, p):
        now, nxt = R[n % 2], R[(n + 1) % 2]
        q = p - 1
        i = q + HU
        m = STEPS - 1 - n

        def chunk(j, carry):
            y8 = pl.multiple_of(j * 8, 8)
            ys = pl.ds(y8, 8)
            ysp = pl.ds(pl.multiple_of(y8 + 8, 8), 8)
            a = [ca[z, i, ys, :] for z in range(2)]
            c = [cc[z, i, ys, :] for z in range(2)]
            layer = [cb[z, i, ys, :] < 1.0 for z in range(2)]
            for s in range(NS):
                w = wavelet[s, m]
                mid, sums = neighbours(now, (s,), p, y8)
                for z in range(2):
                    zs = pl.ds(z * HALF, HALF)
                    old = nxt[s, z, p, ysp, :]
                    new = a[z] * mid[z] - old + c[z] * sums[z] + w * cnt[s, z, q, ys, :]
                    new = jnp.where(layer[z], band[s, m, q, ys, zs], new)
                    nxt[s, z, p, ysp, :] = new
                    band[s, m, q, ys, zs] = (new - mid[z]) - (mid[z] - old)
            return carry

        lax.fori_loop(0, 8, chunk, 0, unroll=8)

    def gather(n):
        ref = F[(n + 1) % 2]
        zero = jnp.zeros((NY, REC), f32)

        def one(p, carry):
            hot = rowhot[pl.ds(pl.multiple_of((p + HU) * NY, NY), NY), :].astype(f32)
            parts = []
            for s in range(NS):
                v = jnp.concatenate([ref[1, s, z, p + 1, data, :] for z in range(2)], axis=1)
                parts.extend(split2(v))
            g = jnp.dot(jnp.concatenate(parts, axis=0), zt[...], preferred_element_type=f32)
            return tuple(
                carry[s] + hot * (g[2 * s * NY : (2 * s + 1) * NY] + g[(2 * s + 1) * NY : (2 * s + 2) * NY])
                for s in range(NS)
            )

        got = lax.fori_loop(0, CX, one, (zero, zero), unroll=8)
        for s in range(NS):
            tr[pl.ds(s * STEPS + n, 1), :] = jnp.sum(got[s], axis=0, keepdims=True)

    def inject(kind, lo, hi):
        def plane(i, carry):
            g = (i + CX - HU) // CX
            hot = rowhot[pl.ds(pl.multiple_of(i * NY, NY), NY), :].astype(f32)
            for s in range(NS):
                parts = []
                for n in range(STEPS):
                    v = amt_s[kind, g, pl.ds(s * STEPS + n, 1), :]
                    v_hi = v.astype(bf16).astype(f32)
                    parts.append(
                        jnp.concatenate(
                            [(hot * v_hi).astype(bf16), (hot * (v - v_hi)).astype(bf16)], axis=1
                        )
                    )
                e = jnp.dot(jnp.concatenate(parts, axis=0), zh2[g], preferred_element_type=f32)
                for n in range(STEPS):
                    E[s * STEPS + n, i] = e[n * NY : (n + 1) * NY]
            return carry

        lax.fori_loop(lo, hi, plane, 0)

    def level(m, img):
        now, nxt = U[(m + 1) % 2], U[m % 2]
        n = STEPS - 1 - m

        def plane(image, i, carry):
            q = i - HU

            def chunk(j, inner):
                y8 = pl.multiple_of(j * 8, 8)
                ys = pl.ds(y8, 8)
                ysp = pl.ds(pl.multiple_of(y8 + 8, 8), 8)
                pic = [None, None]
                for s in range(NS):
                    if m > 0:
                        mid, sums = neighbours(now, (s,), i, y8)
                    for z in range(2):
                        zs = pl.ds(z * HALF, HALF)
                        u = inv[z, i, ys, :] * E[s * STEPS + n, i, ys, zs]
                        if m > 0:
                            u = u + (ca[z, i, ys, :] * mid[z] + cc[z, i, ys, :] * sums[z])
                        if m > 1:
                            u = u - cb[z, i, ys, :] * nxt[s, z, i, ysp, :]
                        if m < STEPS - 1:
                            nxt[s, z, i, ysp, :] = u
                        if image:
                            part = band[s, n, q, ys, pl.ds(z * HALF, HALF)] * u
                            pic[z] = part if s == 0 else pic[z] + part
                if image:
                    for z in range(2):
                        zs = pl.ds(z * HALF, HALF)
                        old = 0.0 if m == 0 else img[q, ys, zs]
                        img[q, ys, zs] = old + pic[z]
                return inner

            lax.fori_loop(0, 8, chunk, 0, unroll=8)
            return carry

        if m < STEPS - 1:
            lax.fori_loop(m, HU, functools.partial(plane, False), 0)
            lax.fori_loop(HU + CX, CU - m, functools.partial(plane, False), 0)
        lax.fori_loop(HU, HU + CX, functools.partial(plane, True), 0, unroll=2)

    def edge_bs(n):
        def one(k, carry):
            step_bs(n, 1 + (CX - 1) * k)
            return carry

        lax.fori_loop(0, 2, one, 0)

    def edge_r(n):
        def one(k, carry):
            step_r(n, 1 + (CX - 1) * k)
            return carry

        lax.fori_loop(0, 2, one, 0)

    def inner_bs(n):
        def one(p, carry):
            step_bs(n, p)
            return carry

        lax.fori_loop(2, CX, one, 0, unroll=2)

    def inner_r(n):
        def one(p, carry):
            step_r(n, p)
            return carry

        lax.fori_loop(2, CX, one, 0, unroll=2)

    for n in range(STEPS):
        if n == 0:
            wait_load("bs1")
            inner_bs(n)
            wait_load("r1")
            inner_r(n)
        bs_faces(n).wait_recv()
        if n > 0:
            bs_faces(n - 1).wait_send()
        edge_bs(n)
        if n < STEPS - 1:
            bs_faces(n + 1).start()
        if n > 0:
            inner_bs(n)
        r_faces(n).wait_recv()
        if n > 0:
            r_faces(n - 1).wait_send()
        edge_r(n)
        if n < STEPS - 1:
            r_faces(n + 1).start()
        if n > 0:
            inner_r(n)
        gather(n)
        if n == 0:
            info_halo.wait_recv()
            c_halo.wait_recv()
            for g, lo in ((0, 0), (1, (HU + CX) * NY)):
                hot_rows(info_n[g, pl.ds(8, 1), :], lo, HU * NY)
                hot_z(info_n[g, pl.ds(9, 1), :], 2 * g)
            lax.fori_loop(0, HU, coef, 0)
            lax.fori_loop(HU + CX, CU, coef, 0)
            amt_s[0, 0] = info_n[0, pl.ds(0, 8), :]
            amt_s[0, 1] = info[pl.ds(0, 8), :]
            amt_s[0, 2] = info_n[1, pl.ds(0, 8), :]
            inject(0, 0, CU)
        level(n, img_r)
    bs_faces(STEPS - 1).wait_send()
    r_faces(STEPS - 1).wait_send()
    info_halo.wait_send()
    c_halo.wait_send()

    def to_shots(r):
        return [
            pltpu.make_async_remote_copy(
                src_ref=ebuf.at[r, 0],
                dst_ref=eslot_s.at[r, me_s],
                send_sem=e_send_s.at[r, d],
                recv_sem=e_recv_s.at[r, d],
                device_id=(lax.rem(me_s + d, n_shot), me_g),
                device_id_type=MESH,
            )
            for d in range(1, n_shot)
        ]

    def to_slabs(r):
        return [
            pltpu.make_async_remote_copy(
                src_ref=ebuf.at[r, 1],
                dst_ref=eslot_g.at[r, me_g],
                send_sem=e_send_g.at[r, d],
                recv_sem=e_recv_g.at[r, d],
                device_id=(me_s, lax.rem(me_g + d, n_gx)),
                device_id_type=MESH,
            )
            for d in range(1, n_gx)
        ]

    def sum_start(value, r):
        ebuf[r, 0] = value
        eslot_s[r, me_s] = value
        for c in to_shots(r):
            c.start()

    def sum_middle(r):
        for c in to_shots(r):
            c.wait_recv()
        total = eslot_s[r, 0]
        for d in range(1, n_shot):
            total = total + eslot_s[r, d]
        ebuf[r, 1] = total
        eslot_g[r, me_g] = total
        for c in to_slabs(r):
            c.start()

    def sum_end(r):
        for c in to_slabs(r):
            c.wait_recv()
        total = eslot_g[r, 0]
        for d in range(1, n_gx):
            total = total + eslot_g[r, d]
        return jnp.sum(total)

    t = tr[...]
    tr_halo.start()
    sum_start(t * t, 0)
    amt_s[1, 1] = t
    inject(1, HU, HU + CX)
    tr_halo.wait_recv()
    amt_s[1, 0] = tr_n[0]
    amt_s[1, 2] = tr_n[1]
    inject(1, 0, HU)
    inject(1, HU + CX, CU)
    level(0, img_t)
    sum_middle(0)
    for m in range(1, STEPS):
        level(m, img_t)
    energy = sum_end(0)
    gn = jnp.full((8, HALF), grad_norm[0], f32)
    step = gn / (jnp.full((8, HALF), energy, f32) + tiny)
    for s in range(NS):
        resid_o[s] = residual[s] - step[0:STEPS] * t[s * STEPS : (s + 1) * STEPS]

    def combine(q):
        for y in range(8):
            ys = pl.ds(y * 8, 8)
            for z in range(2):
                zs = pl.ds(z * HALF, HALF)
                img_r[q, ys, zs] = c0[z, HU + q, ys, :] * (
                    step * img_t[q, ys, zs] - img_r[q, ys, zs]
                )

    scatter = []
    for d in range(1, n_shot):
        to = lax.rem(me_s + d, n_shot)
        combine(to)
        c = pltpu.make_async_remote_copy(
            src_ref=img_r.at[to],
            dst_ref=rs.at[d - 1],
            send_sem=g_send.at[0, d],
            recv_sem=g_recv.at[0, d],
            device_id=(to, me_g),
            device_id_type=MESH,
        )
        c.start()
        scatter.append(c)
    combine(me_s)
    for c in scatter:
        c.wait_recv()

    def add(i, carry):
        ys = pl.ds(pl.multiple_of(i * 8, 8), 8)
        g = img_r[me_s, ys, :]
        for d in range(1, n_shot):
            g = g + rs[d - 1, ys, :]
        grad_o[me_s, ys, :] = g
        g = g * g
        return carry + (g[:, :HALF] + g[:, HALF:])

    part = lax.fori_loop(0, 8, add, jnp.zeros((8, HALF), f32), unroll=8)
    sum_start(part, 1)
    spread = []
    for d in range(1, n_shot):
        to = lax.rem(me_s + d, n_shot)
        c = pltpu.make_async_remote_copy(
            src_ref=grad_o.at[me_s],
            dst_ref=grad_o.at[me_s],
            send_sem=g_send.at[1, d],
            recv_sem=g_recv.at[1, d],
            device_id=(to, me_g),
            device_id_type=MESH,
        )
        c.start()
        spread.append(c)
    sum_middle(1)
    grad_energy = sum_end(1)
    ratio = jnp.full((8, HALF), grad_energy, f32) / gn
    scal_o[pl.ds(0, 8), :] = step
    scal_o[pl.ds(8, 8), :] = ratio
    for d in range(1, n_shot):
        came = lax.rem(me_s + n_shot - d, n_shot)
        pltpu.make_async_remote_copy(
            src_ref=grad_o.at[came],
            dst_ref=grad_o.at[came],
            send_sem=g_send.at[1, d],
            recv_sem=g_recv.at[1, d],
            device_id=(came, me_g),
            device_id_type=MESH,
        ).wait_recv()
    tr_halo.wait_send()
    for r in range(2):
        for c in to_shots(r) + to_slabs(r):
            c.wait_send()
    for c in scatter + spread:
        c.wait_send()


def finish(scal, gradient, direction, model_image, resid, image_o, dir_o, resid_o, image, out, sem):
    step = scal[0:1, 0:1]
    ratio = scal[8:9, 0:1]
    copies = [pltpu.make_async_copy(resid, resid_o, sem.at[0])]
    copies[0].start()
    half = CX // 2
    for k in range(2):
        ps = pl.ds(k * half, half)

        def plane(p, carry):
            d = direction[p]
            image[p] = model_image[p] + step * d
            out[p] = gradient[p] + ratio * d
            return carry

        lax.fori_loop(k * half, (k + 1) * half, plane, 0)
        for b, (src, dst) in enumerate(((image, image_o), (out, dir_o))):
            c = pltpu.make_async_copy(src.at[ps], dst.at[ps], sem.at[1 + 2 * k + b])
            c.start()
            copies.append(c)
    for c in copies:
        c.wait()


def per_device(
    n_shot,
    n_gx,
    courant,
    absorb,
    model_image,
    direction,
    back_prev,
    back_now,
    scat_prev,
    scat_now,
    back_end,
    back_before_end,
    back_band,
    src_pos,
    wavelet,
    rec_pos,
    residual,
    grad_norm,
):
    hbm = pl.BlockSpec(memory_space=pl.ANY)
    vmem = pl.BlockSpec(memory_space=pltpu.VMEM)
    smem = pl.BlockSpec(memory_space=pltpu.SMEM)
    slab = (2, CX, NY, HALF)
    wide = (2, CU, NY, HALF)
    dma = pltpu.SemaphoreType.DMA
    V = pltpu.VMEM
    gradient, resid, scal = pl.pallas_call(
        functools.partial(kernel, n_shot, n_gx),
        out_shape=(
            jax.ShapeDtypeStruct((CX, NY, NZ), f32),
            jax.ShapeDtypeStruct((NS, STEPS, REC), f32),
            jax.ShapeDtypeStruct((16, HALF), f32),
        ),
        in_specs=[hbm] * 9 + [smem] * 3 + [vmem] * 3,
        out_specs=(vmem, vmem, vmem),
        scratch_shapes=[
            V((2, NS, 2, CX + 2, PY, HALF), f32),
            V((2, NS, 2, CX + 2, PY, HALF), f32),
            V((NS, 2, CX + 2, PY, HALF), f32),
            V((NS, 2, CX + 2, PY, HALF), f32),
            V((NS, 2, CU, PY, HALF), f32),
            V((NS, 2, CU, PY, HALF), f32),
            V((NS, STEPS, CX, NY, NZ), f32),
            V(wide, f32),
            V(slab, f32),
            V(wide, f32),
            V(wide, f32),
            V(wide, f32),
            V(wide, f32),
            V((NS,) + slab, f32),
            V((CU * NY, REC), bf16),
            V((NZ, REC), bf16),
            V((3, 2 * REC, NZ), bf16),
            V((16, REC), f32),
            V((2, 16, REC), f32),
            V((NS * STEPS, REC), f32),
            V((2, NS * STEPS, REC), f32),
            V((2, 3, NS * STEPS, REC), f32),
            V((NS * STEPS, CU, NY, NZ), f32),
            V((CX, NY, NZ), f32),
            V((CX, NY, NZ), f32),
            V((n_shot - 1, NY, NZ), f32),
            V((2, 2, 8, HALF), f32),
            V((2, n_shot, 8, HALF), f32),
            V((2, n_gx, 8, HALF), f32),
            dma((17,)),
            dma((STEPS, 2)),
            dma((STEPS, 2)),
            dma((STEPS, 2)),
            dma((STEPS, 2)),
            dma((3, 2)),
            dma((3, 2)),
            dma((2, n_shot)),
            dma((2, n_shot)),
            dma((2, n_gx)),
            dma((2, n_gx)),
            dma((2, n_shot)),
            dma((2, n_shot)),
        ],
        compiler_params=pltpu.CompilerParams(
            collective_id=0,
            has_side_effects=True,
            vmem_limit_bytes=58 * 1024 * 1024,
        ),
        name="lsrtm",
    )(
        courant,
        direction,
        back_prev,
        back_now,
        scat_prev,
        scat_now,
        back_end,
        back_before_end,
        back_band,
        absorb,
        wavelet,
        grad_norm,
        jnp.transpose(src_pos, (2, 0, 1)),
        jnp.transpose(rec_pos, (2, 0, 1)),
        residual,
    )
    return pl.pallas_call(
        finish,
        out_shape=[
            jax.ShapeDtypeStruct((CX, NY, NZ), f32),
            jax.ShapeDtypeStruct((CX, NY, NZ), f32),
            jax.ShapeDtypeStruct((NS, STEPS, REC), f32),
        ],
        in_specs=[vmem] * 5,
        out_specs=[pl.BlockSpec(memory_space=pltpu.HBM)] * 3,
        scratch_shapes=[V((CX, NY, NZ), f32), V((CX, NY, NZ), f32), dma((5,))],
        compiler_params=pltpu.CompilerParams(vmem_limit_bytes=16 * 1024 * 1024),
        name="finish",
    )(scal, gradient, direction, model_image, resid)


def solution(mesh):
    field = P("shot", "gx", None, None)
    grid = P("gx", None, None)
    in_specs = (
        grid,
        P(),
        grid,
        grid,
        field,
        field,
        field,
        field,
        field,
        field,
        P("shot", None, "gx", None, None),
        P("shot", None, None),
        P("shot", None),
        P("shot", "gx", None),
        P("shot", None, "gx"),
        P(),
    )
    return jax.shard_map(
        functools.partial(per_device, mesh.shape["shot"], mesh.shape["gx"]),
        mesh=mesh,
        in_specs=in_specs,
        out_specs=(grid, grid, P("shot", None, "gx")),
        check_vma=False,
    )
```

```python
import functools

import jax
import jax.numpy as jnp
from jax import lax
from jax.experimental import pallas as pl
from jax.experimental.pallas import tpu as pltpu
from jax.sharding import PartitionSpec as P

damp_peak = 0.4
tiny = 1e-6
CX, NY, NZ = 8, 64, 256
NS, STEPS, REC, SRC = 2, 4, 128, 64
PY = 80
HU = 3
CU = CX + 2 * HU
HALF = 128
MESH = pl.DeviceIdType.MESH
f32 = jnp.float32
bf16 = jnp.bfloat16


def split2(v):
    hi = v.astype(bf16)
    lo = (v - hi.astype(f32)).astype(bf16)
    return hi, lo


def profile(pos, extent, low, high):
    gap = extent - 1 - pos
    low_f = low.astype(f32)
    high_f = high.astype(f32)
    near_low = jnp.where(pos < low, ((low - pos).astype(f32) / low_f) ** 2, 0.0)
    near_high = jnp.where(gap < high, ((high - gap).astype(f32) / high_f) ** 2, 0.0)
    return damp_peak * (near_low + near_high)


def kernel(
    n_shot,
    n_gx,
    courant_h,
    direction_h,
    back_prev_h,
    back_now_h,
    scat_prev_h,
    scat_now_h,
    back_end_h,
    back_before_h,
    band_h,
    absorb,
    wavelet,
    grad_norm,
    src_pos,
    rec_pos,
    residual,
    grad_o,
    resid_o,
    scal_o,
    F0,
    F1,
    R0,
    R1,
    U0,
    U1,
    band,
    c0,
    dirv,
    ca,
    cb,
    cc,
    inv,
    cnt,
    rowhot,
    zt,
    zh2,
    info,
    info_n,
    tr,
    tr_n,
    amt_s,
    E,
    img_r,
    img_t,
    rs,
    ebuf,
    eslot_s,
    eslot_g,
    ld_sem,
    f_send,
    f_recv,
    r_send,
    r_recv,
    h_send,
    h_recv,
    e_send_s,
    e_recv_s,
    e_send_g,
    e_recv_g,
    g_send,
    g_recv,
):
    me_s = lax.axis_index("shot")
    me_g = lax.axis_index("gx")
    has_left = me_g > 0
    has_right = me_g < n_gx - 1
    F = (F0, F1)
    R = (R0, R1)
    U = (U0, U1)
    own = pl.ds(HU, CX)
    data = pl.ds(8, NY)
    every = slice(None)

    loads = {}
    count_l = [0]

    def load(name, src, dst):
        c = pltpu.make_async_copy(src, dst, ld_sem.at[count_l[0]])
        count_l[0] += 1
        c.start()
        loads.setdefault(name, []).append(c)

    def wait_load(name):
        for c in loads[name]:
            c.wait()

    def load_field(name, src, dst):
        for z in range(2):
            load(name, src.at[:, :, :, pl.ds(z * HALF, HALF)], dst.at[:, z, pl.ds(1, CX), data, :])

    load_field("b0", back_now_h, F0.at[0])
    load_field("s0", scat_now_h, F0.at[1])
    load_field("r0", back_before_h, R0)
    for z in range(2):
        load("c", courant_h.at[:, :, pl.ds(z * HALF, HALF)], c0.at[z, own])
    load_field("bs1", back_prev_h, F1.at[0])
    load_field("bs1", scat_prev_h, F1.at[1])
    for z in range(2):
        load("bs1", direction_h.at[:, :, pl.ds(z * HALF, HALF)], dirv.at[z])
    load_field("r1", back_end_h, R1)
    load("r1", band_h, band)

    zero8 = jnp.zeros((8, HALF), f32)
    zero64 = jnp.zeros((NY, HALF), f32)
    lead_f = [(f, s, z) for f in range(2) for s in range(NS) for z in range(2)]
    lead_r = [(s, z) for s in range(NS) for z in range(2)]
    for p in (0, CX + 1):
        for b in range(2):
            for idx in lead_f:
                F[b][idx + (p, data, every)] = zero64
            for idx in lead_r:
                R[b][idx + (p, data, every)] = zero64
    for z in range(2):
        for p in range(HU):
            c0[z, p] = zero64
            c0[z, HU + CX + p] = zero64
    for g in range(2):
        info_n[g, pl.ds(0, 8), :] = zero8
        info_n[g, pl.ds(8, 8), :] = zero8
        tr_n[g] = zero8

    bar = pltpu.get_barrier_semaphore()
    for d in range(1, n_gx):
        pl.semaphore_signal(
            bar, inc=1, device_id=(me_s, lax.rem(me_g + d, n_gx)), device_id_type=MESH
        )
    for d in range(1, n_shot):
        pl.semaphore_signal(
            bar, inc=1, device_id=(lax.rem(me_s + d, n_shot), me_g), device_id_type=MESH
        )

    rec_row = (rec_pos[0, 0:1, :] * NY + rec_pos[1, 0:1, :]).astype(f32)
    rec_z = rec_pos[2, 0:1, :].astype(f32)
    for s in range(NS):
        info[pl.ds(s * STEPS, STEPS), :] = residual[s]
    info[pl.ds(8, 1), :] = rec_row
    info[pl.ds(9, 1), :] = rec_z
    info[pl.ds(10, 6), :] = jnp.zeros((6, REC), f32)

    class Pair:
        def __init__(self, to_left, to_right, send, recv):
            self.refs = (to_left, to_right)
            self.send = send
            self.recv = recv

        def copy(self, side):
            src, dst = self.refs[side]
            return pltpu.make_async_remote_copy(
                src_ref=src,
                dst_ref=dst,
                send_sem=self.send.at[side],
                recv_sem=self.recv.at[side],
                device_id=(me_s, me_g - 1 if side == 0 else me_g + 1),
                device_id_type=MESH,
            )

        def start(self):
            @pl.when(has_left)
            def _():
                self.copy(0).start()

            @pl.when(has_right)
            def _():
                self.copy(1).start()

        def wait_recv(self):
            @pl.when(has_right)
            def _():
                self.copy(0).wait_recv()

            @pl.when(has_left)
            def _():
                self.copy(1).wait_recv()

        def wait_send(self):
            @pl.when(has_left)
            def _():
                self.copy(0).wait_send()

            @pl.when(has_right)
            def _():
                self.copy(1).wait_send()

    def face(buf, lead, p):
        return buf.at[(every,) * lead + (p, data, every)]

    def bs_faces(n, s):
        b = F[n % 2]
        return Pair(
            (b.at[:, s, :, 1, data, :], b.at[:, s, :, CX + 1, data, :]),
            (b.at[:, s, :, CX, data, :], b.at[:, s, :, 0, data, :]),
            f_send.at[n, s],
            f_recv.at[n, s],
        )

    def r_faces(n):
        b = R[n % 2]
        return Pair(
            (face(b, 2, 1), face(b, 2, CX + 1)),
            (face(b, 2, CX), face(b, 2, 0)),
            r_send.at[n],
            r_recv.at[n],
        )

    c_halo = Pair(
        (c0.at[:, pl.ds(HU, HU)], c0.at[:, pl.ds(HU + CX, HU)]),
        (c0.at[:, pl.ds(CX, HU)], c0.at[:, pl.ds(0, HU)]),
        h_send.at[0],
        h_recv.at[0],
    )
    info_halo = Pair((info, info_n.at[1]), (info, info_n.at[0]), h_send.at[1], h_recv.at[1])
    tr_halo = Pair((tr, tr_n.at[1]), (tr, tr_n.at[0]), h_send.at[2], h_recv.at[2])

    def pads(p, carry):
        for b in range(2):
            for idx in lead_f:
                F[b][idx + (p, pl.ds(0, 8), every)] = zero8
                F[b][idx + (p, pl.ds(72, 8), every)] = zero8
            for idx in lead_r:
                R[b][idx + (p, pl.ds(0, 8), every)] = zero8
                R[b][idx + (p, pl.ds(72, 8), every)] = zero8
        return carry

    lax.fori_loop(0, CX + 2, pads, 0)

    def pads_u(p, carry):
        for b in range(2):
            for idx in lead_r:
                U[b][idx + (p, pl.ds(0, 8), every)] = zero8
                U[b][idx + (p, pl.ds(72, 8), every)] = zero8
        return carry

    lax.fori_loop(0, CU, pads_u, 0)

    def to_col(row, n):
        eye = lax.broadcasted_iota(jnp.int32, (n, n), 0) == lax.broadcasted_iota(
            jnp.int32, (n, n), 1
        )
        return jnp.sum(jnp.where(eye, row, 0.0), axis=1, keepdims=True)

    first_row = ((me_g * CX - HU) * NY).astype(f32)

    def hot_rows(row, lo, n):
        rows = lax.broadcasted_iota(jnp.int32, (n, REC), 0).astype(f32) + (first_row + lo)
        rowhot[pl.ds(lo, n), :] = jnp.where(rows == row, 1.0, 0.0).astype(bf16)

    lane_z = lax.broadcasted_iota(jnp.int32, (REC, NZ), 1).astype(f32)

    def hot_z(z_row, g):
        hot = jnp.where(lane_z == to_col(z_row, REC), 1.0, 0.0).astype(bf16)
        zh2[g, pl.ds(0, REC), :] = hot
        zh2[g, pl.ds(REC, REC), :] = hot

    hot_rows(rec_row, HU * NY, CX * NY)
    hot_z(rec_z, 1)
    zt[...] = jnp.where(
        lax.broadcasted_iota(jnp.int32, (NZ, REC), 0).astype(f32) == rec_z, 1.0, 0.0
    ).astype(bf16)

    pl.semaphore_wait(bar, n_gx - 1 + n_shot - 1)
    wait_load("b0")
    wait_load("s0")
    for s in range(NS):
        bs_faces(0, s).start()
    wait_load("r0")
    r_faces(0).start()
    info_halo.start()
    wait_load("c")
    c_halo.start()

    nx = n_gx * CX
    lane = lax.broadcasted_iota(jnp.int32, (8, HALF), 1)
    sub = lax.broadcasted_iota(jnp.int32, (8, HALF), 0)
    damp_z = [profile(lane + z * HALF, NZ, absorb[4], absorb[5]) for z in range(2)]

    def coef(i, carry):
        pos_x = jnp.full((8, HALF), me_g * CX - HU + i, jnp.int32)
        damp_x = profile(pos_x, nx, absorb[0], absorb[1])
        for y in range(8):
            ys = pl.ds(y * 8, 8)
            damp_xy = damp_x + profile(sub + y * 8, NY, absorb[2], absorb[3])
            for z in range(2):
                damping = damp_xy + damp_z[z]
                c = c0[z, i, ys, :]
                iv = 1.0 / (1.0 + damping)
                inv[z, i, ys, :] = iv
                ca[z, i, ys, :] = (2.0 - 6.0 * c) * iv
                cb[z, i, ys, :] = (1.0 - damping) * iv
                cc[z, i, ys, :] = c * iv
        return carry

    lax.fori_loop(HU, HU + CX, coef, 0)

    src_hot = []
    for s in range(NS):
        s_row = ((src_pos[0, s : s + 1, :] - me_g * CX) * NY + src_pos[1, s : s + 1, :]).astype(
            f32
        )
        s_z = to_col(src_pos[2, s : s + 1, :].astype(f32), SRC)
        s_hot = jnp.where(
            lax.broadcasted_iota(jnp.int32, (SRC, NZ), 1).astype(f32) == s_z, 1.0, 0.0
        ).astype(bf16)
        src_hot.append((s_row, s_hot))

    def count(p, carry):
        rows = (lax.broadcasted_iota(jnp.int32, (NY, SRC), 0) + p * NY).astype(f32)
        for s in range(NS):
            hot = jnp.where(rows == src_hot[s][0], 1.0, 0.0).astype(bf16)
            n = jnp.dot(hot, src_hot[s][1], preferred_element_type=f32)
            for z in range(2):
                cnt[s, z, p] = n[:, z * HALF : (z + 1) * HALF] * inv[z, HU + p]
        return carry

    lax.fori_loop(0, CX, count, 0, unroll=2)

    first = lane == 0
    last = lane == HALF - 1

    def neighbours(ref, lead, p, y8):
        ys = pl.ds(8 + y8, 8)
        mid = [ref[lead + (z, p, ys, every)] for z in range(2)]
        right = [pltpu.roll(m, 1, 1) for m in mid]
        left = [pltpu.roll(m, HALF - 1, 1) for m in mid]
        low = [jnp.where(first, 0.0, right[0]), jnp.where(first, right[0], right[1])]
        high = [jnp.where(last, left[1], left[0]), jnp.where(last, 0.0, left[1])]
        sums = []
        for z in range(2):
            t = ref[lead + (z, p + 1, ys, every)] + ref[lead + (z, p - 1, ys, every)]
            t = t + (
                ref[lead + (z, p, pl.ds(y8 + 9, 8), every)]
                + ref[lead + (z, p, pl.ds(y8 + 7, 8), every)]
            )
            sums.append(t + (low[z] + high[z]))
        return mid, sums

    def step_bs(n, p, shots):
        now, nxt = F[n % 2], F[(n + 1) % 2]
        q = p - 1
        i = q + HU

        def chunk(j, carry):
            y8 = pl.multiple_of(j * 8, 8)
            ys = pl.ds(y8, 8)
            ysp = pl.ds(pl.multiple_of(y8 + 8, 8), 8)
            a = [ca[z, i, ys, :] for z in range(2)]
            b = [cb[z, i, ys, :] for z in range(2)]
            c = [cc[z, i, ys, :] for z in range(2)]
            di = [dirv[z, q, ys, :] for z in range(2)]
            for s in shots:
                w = wavelet[s, n]
                mid, sums = neighbours(now, (0, s), p, y8)
                acc = []
                for z in range(2):
                    old = nxt[0, s, z, p, ysp, :]
                    new = (
                        a[z] * mid[z]
                        - b[z] * old
                        + c[z] * sums[z]
                        + w * cnt[s, z, q, ys, :]
                    )
                    nxt[0, s, z, p, ysp, :] = new
                    acc.append((new - mid[z]) - (mid[z] - old))
                mid, sums = neighbours(now, (1, s), p, y8)
                for z in range(2):
                    old = nxt[1, s, z, p, ysp, :]
                    nxt[1, s, z, p, ysp, :] = (
                        a[z] * mid[z] - b[z] * old + c[z] * (sums[z] - di[z] * acc[z])
                    )
            return carry

        lax.fori_loop(0, 8, chunk, 0, unroll=8)

    def step_r(n, p):
        now, nxt = R[n % 2], R[(n + 1) % 2]
        q = p - 1
        i = q + HU
        m = STEPS - 1 - n

        def chunk(j, carry):
            y8 = pl.multiple_of(j * 8, 8)
            ys = pl.ds(y8, 8)
            ysp = pl.ds(pl.multiple_of(y8 + 8, 8), 8)
            a = [ca[z, i, ys, :] for z in range(2)]
            c = [cc[z, i, ys, :] for z in range(2)]
            layer = [cb[z, i, ys, :] < 1.0 for z in range(2)]
            for s in range(NS):
                w = wavelet[s, m]
                mid, sums = neighbours(now, (s,), p, y8)
                for z in range(2):
                    zs = pl.ds(z * HALF, HALF)
                    old = nxt[s, z, p, ysp, :]
                    new = a[z] * mid[z] - old + c[z] * sums[z] + w * cnt[s, z, q, ys, :]
                    new = jnp.where(layer[z], band[s, m, q, ys, zs], new)
                    nxt[s, z, p, ysp, :] = new
                    band[s, m, q, ys, zs] = (new - mid[z]) - (mid[z] - old)
            return carry

        lax.fori_loop(0, 8, chunk, 0, unroll=8)

    def gather(n):
        ref = F[(n + 1) % 2]
        zero = jnp.zeros((NY, REC), f32)

        def one(p, carry):
            hot = rowhot[pl.ds(pl.multiple_of((p + HU) * NY, NY), NY), :].astype(f32)
            parts = []
            for s in range(NS):
                v = jnp.concatenate([ref[1, s, z, p + 1, data, :] for z in range(2)], axis=1)
                parts.extend(split2(v))
            g = jnp.dot(jnp.concatenate(parts, axis=0), zt[...], preferred_element_type=f32)
            return tuple(
                carry[s] + hot * (g[2 * s * NY : (2 * s + 1) * NY] + g[(2 * s + 1) * NY : (2 * s + 2) * NY])
                for s in range(NS)
            )

        got = lax.fori_loop(0, CX, one, (zero, zero), unroll=8)
        for s in range(NS):
            tr[pl.ds(s * STEPS + n, 1), :] = jnp.sum(got[s], axis=0, keepdims=True)

    def inject(kind, lo, hi):
        def plane(i, carry):
            g = (i + CX - HU) // CX
            hot = rowhot[pl.ds(pl.multiple_of(i * NY, NY), NY), :].astype(f32)
            for s in range(NS):
                parts = []
                for n in range(STEPS):
                    v = amt_s[kind, g, pl.ds(s * STEPS + n, 1), :]
                    v_hi = v.astype(bf16).astype(f32)
                    parts.append(
                        jnp.concatenate(
                            [(hot * v_hi).astype(bf16), (hot * (v - v_hi)).astype(bf16)], axis=1
                        )
                    )
                e = jnp.dot(jnp.concatenate(parts, axis=0), zh2[g], preferred_element_type=f32)
                for n in range(STEPS):
                    E[s * STEPS + n, i] = e[n * NY : (n + 1) * NY]
            return carry

        lax.fori_loop(lo, hi, plane, 0)

    def level(m, img):
        now, nxt = U[(m + 1) % 2], U[m % 2]
        n = STEPS - 1 - m

        def plane(image, i, carry):
            q = i - HU

            def chunk(j, inner):
                y8 = pl.multiple_of(j * 8, 8)
                ys = pl.ds(y8, 8)
                ysp = pl.ds(pl.multiple_of(y8 + 8, 8), 8)
                pic = [None, None]
                for s in range(NS):
                    if m > 0:
                        mid, sums = neighbours(now, (s,), i, y8)
                    for z in range(2):
                        zs = pl.ds(z * HALF, HALF)
                        u = inv[z, i, ys, :] * E[s * STEPS + n, i, ys, zs]
                        if m > 0:
                            u = u + (ca[z, i, ys, :] * mid[z] + cc[z, i, ys, :] * sums[z])
                        if m > 1:
                            u = u - cb[z, i, ys, :] * nxt[s, z, i, ysp, :]
                        if m < STEPS - 1:
                            nxt[s, z, i, ysp, :] = u
                        if image:
                            part = band[s, n, q, ys, pl.ds(z * HALF, HALF)] * u
                            pic[z] = part if s == 0 else pic[z] + part
                if image:
                    for z in range(2):
                        zs = pl.ds(z * HALF, HALF)
                        old = 0.0 if m == 0 else img[q, ys, zs]
                        img[q, ys, zs] = old + pic[z]
                return inner

            lax.fori_loop(0, 8, chunk, 0, unroll=8)
            return carry

        if m < STEPS - 1:
            lax.fori_loop(m, HU, functools.partial(plane, False), 0)
            lax.fori_loop(HU + CX, CU - m, functools.partial(plane, False), 0)
        lax.fori_loop(HU, HU + CX, functools.partial(plane, True), 0, unroll=2)

    def edge_bs(n, s):
        def one(k, carry):
            step_bs(n, 1 + (CX - 1) * k, (s,))
            return carry

        lax.fori_loop(0, 2, one, 0, unroll=2)

    def edge_r(n):
        def one(k, carry):
            step_r(n, 1 + (CX - 1) * k)
            return carry

        lax.fori_loop(0, 2, one, 0)

    def inner_bs(n, shots):
        def one(p, carry):
            step_bs(n, p, shots)
            return carry

        lax.fori_loop(2, CX, one, 0, unroll=2)

    def inner_r(n):
        def one(p, carry):
            step_r(n, p)
            return carry

        lax.fori_loop(2, CX, one, 0, unroll=2)

    for n in range(STEPS):
        if n == 0:
            wait_load("bs1")
            inner_bs(n, range(NS))
            wait_load("r1")
            inner_r(n)
        for s in range(NS):
            bs_faces(n, s).wait_recv()
            if n > 0:
                bs_faces(n - 1, s).wait_send()
            edge_bs(n, s)
            if n < STEPS - 1:
                bs_faces(n + 1, s).start()
            if n > 0:
                inner_bs(n, (s,))
        r_faces(n).wait_recv()
        if n > 0:
            r_faces(n - 1).wait_send()
        edge_r(n)
        if n < STEPS - 1:
            r_faces(n + 1).start()
        if n > 0:
            inner_r(n)
        gather(n)
        if n == 0:
            info_halo.wait_recv()
            c_halo.wait_recv()
            for g, lo in ((0, 0), (1, (HU + CX) * NY)):
                hot_rows(info_n[g, pl.ds(8, 1), :], lo, HU * NY)
                hot_z(info_n[g, pl.ds(9, 1), :], 2 * g)
            lax.fori_loop(0, HU, coef, 0)
            lax.fori_loop(HU + CX, CU, coef, 0)
            amt_s[0, 0] = info_n[0, pl.ds(0, 8), :]
            amt_s[0, 1] = info[pl.ds(0, 8), :]
            amt_s[0, 2] = info_n[1, pl.ds(0, 8), :]
            inject(0, 0, CU)
        level(n, img_r)
    for s in range(NS):
        bs_faces(STEPS - 1, s).wait_send()
    r_faces(STEPS - 1).wait_send()
    info_halo.wait_send()
    c_halo.wait_send()

    def to_slabs(r):
        return [
            pltpu.make_async_remote_copy(
                src_ref=ebuf.at[r, 0],
                dst_ref=eslot_g.at[r, me_g],
                send_sem=e_send_g.at[r, d],
                recv_sem=e_recv_g.at[r, d],
                device_id=(me_s, lax.rem(me_g + d, n_gx)),
                device_id_type=MESH,
            )
            for d in range(1, n_gx)
        ]

    def to_shots(r):
        return [
            pltpu.make_async_remote_copy(
                src_ref=ebuf.at[r, 1],
                dst_ref=eslot_s.at[r, me_s],
                send_sem=e_send_s.at[r, d],
                recv_sem=e_recv_s.at[r, d],
                device_id=(lax.rem(me_s + d, n_shot), me_g),
                device_id_type=MESH,
            )
            for d in range(1, n_shot)
        ]

    def sum_start(value, r):
        ebuf[r, 0] = value
        eslot_g[r, me_g] = value
        for c in to_slabs(r):
            c.start()

    def sum_middle(r):
        for c in to_slabs(r):
            c.wait_recv()
        total = eslot_g[r, 0]
        for d in range(1, n_gx):
            total = total + eslot_g[r, d]
        ebuf[r, 1] = total
        eslot_s[r, me_s] = total
        for c in to_shots(r):
            c.start()

    def sum_end(r):
        for c in to_shots(r):
            c.wait_recv()
        total = eslot_s[r, 0]
        for d in range(1, n_shot):
            total = total + eslot_s[r, d]
        return jnp.sum(total)

    t = tr[...]
    tr_halo.start()
    sum_start(t * t, 0)
    amt_s[1, 1] = t
    inject(1, HU, HU + CX)
    tr_halo.wait_recv()
    amt_s[1, 0] = tr_n[0]
    amt_s[1, 2] = tr_n[1]
    inject(1, 0, HU)
    inject(1, HU + CX, CU)
    level(0, img_t)
    sum_middle(0)
    for m in range(1, STEPS - 1):
        level(m, img_t)
    energy = sum_end(0)
    gn = jnp.full((8, HALF), grad_norm[0], f32)
    step = gn / (jnp.full((8, HALF), energy, f32) + tiny)
    for s in range(NS):
        resid_o[s] = residual[s] - step[0:STEPS] * t[s * STEPS : (s + 1) * STEPS]

    def to_sum(d):
        to = lax.rem(me_s + d, n_shot)
        return pltpu.make_async_remote_copy(
            src_ref=img_r.at[to],
            dst_ref=rs.at[d - 1],
            send_sem=g_send.at[0, d],
            recv_sem=g_recv.at[0, d],
            device_id=(to, me_g),
            device_id_type=MESH,
        )

    m_last = STEPS - 1
    now_u, old_u = U[(m_last + 1) % 2], U[m_last % 2]

    def gradient_plane(d, carry):
        q = lax.rem(me_s + d, n_shot)
        i = q + HU

        def chunk(j, inner):
            y8 = pl.multiple_of(j * 8, 8)
            ys = pl.ds(y8, 8)
            ysp = pl.ds(pl.multiple_of(y8 + 8, 8), 8)
            pic = [img_t[q, ys, pl.ds(z * HALF, HALF)] for z in range(2)]
            for s in range(NS):
                mid, sums = neighbours(now_u, (s,), i, y8)
                for z in range(2):
                    zs = pl.ds(z * HALF, HALF)
                    u = inv[z, i, ys, :] * E[s * STEPS, i, ys, zs]
                    u = u + (ca[z, i, ys, :] * mid[z] + cc[z, i, ys, :] * sums[z])
                    u = u - cb[z, i, ys, :] * old_u[s, z, i, ysp, :]
                    pic[z] = pic[z] + band[s, 0, q, ys, zs] * u
            for z in range(2):
                zs = pl.ds(z * HALF, HALF)
                img_r[q, ys, zs] = c0[z, i, ys, :] * (step * pic[z] - img_r[q, ys, zs])
            return inner

        lax.fori_loop(0, 8, chunk, 0, unroll=8)

        @pl.when(d < n_shot)
        def _():
            to_sum(d).start()

        return carry

    lax.fori_loop(1, n_shot + 1, gradient_plane, 0)
    for d in range(1, n_shot):
        to_sum(d).wait_recv()

    def add(i, carry):
        ys = pl.ds(pl.multiple_of(i * 8, 8), 8)
        g = img_r[me_s, ys, :]
        for d in range(1, n_shot):
            g = g + rs[d - 1, ys, :]
        grad_o[me_s, ys, :] = g
        g = g * g
        return carry + (g[:, :HALF] + g[:, HALF:])

    part = lax.fori_loop(0, 8, add, jnp.zeros((8, HALF), f32), unroll=8)
    sum_start(part, 1)
    def spread(d):
        return pltpu.make_async_remote_copy(
            src_ref=grad_o.at[me_s],
            dst_ref=grad_o.at[me_s],
            send_sem=g_send.at[1, d],
            recv_sem=g_recv.at[1, d],
            device_id=(lax.rem(me_s + d, n_shot), me_g),
            device_id_type=MESH,
        )

    for d in range(1, n_shot, 2):
        spread(d).start()
    sum_middle(1)
    for d in range(2, n_shot, 2):
        spread(d).start()
    grad_energy = sum_end(1)
    ratio = jnp.full((8, HALF), grad_energy, f32) / gn
    scal_o[pl.ds(0, 8), :] = step
    scal_o[pl.ds(8, 8), :] = ratio
    for d in range(1, n_shot):
        came = lax.rem(me_s + n_shot - d, n_shot)
        pltpu.make_async_remote_copy(
            src_ref=grad_o.at[came],
            dst_ref=grad_o.at[came],
            send_sem=g_send.at[1, d],
            recv_sem=g_recv.at[1, d],
            device_id=(came, me_g),
            device_id_type=MESH,
        ).wait_recv()
    tr_halo.wait_send()
    for r in range(2):
        for c in to_shots(r) + to_slabs(r):
            c.wait_send()
    for d in range(1, n_shot):
        to_sum(d).wait_send()
        spread(d).wait_send()


def finish(scal, gradient, direction, model_image, resid, image_o, dir_o, resid_o, image, out, sem):
    step = scal[0:1, 0:1]
    ratio = scal[8:9, 0:1]
    copies = [pltpu.make_async_copy(resid, resid_o, sem.at[0])]
    copies[0].start()
    half = CX // 2
    for k in range(2):
        ps = pl.ds(k * half, half)

        def plane(p, carry):
            d = direction[p]
            image[p] = model_image[p] + step * d
            out[p] = gradient[p] + ratio * d
            return carry

        lax.fori_loop(k * half, (k + 1) * half, plane, 0)
        for b, (src, dst) in enumerate(((image, image_o), (out, dir_o))):
            c = pltpu.make_async_copy(src.at[ps], dst.at[ps], sem.at[1 + 2 * k + b])
            c.start()
            copies.append(c)
    for c in copies:
        c.wait()


def per_device(
    n_shot,
    n_gx,
    courant,
    absorb,
    model_image,
    direction,
    back_prev,
    back_now,
    scat_prev,
    scat_now,
    back_end,
    back_before_end,
    back_band,
    src_pos,
    wavelet,
    rec_pos,
    residual,
    grad_norm,
):
    hbm = pl.BlockSpec(memory_space=pl.ANY)
    vmem = pl.BlockSpec(memory_space=pltpu.VMEM)
    smem = pl.BlockSpec(memory_space=pltpu.SMEM)
    slab = (2, CX, NY, HALF)
    wide = (2, CU, NY, HALF)
    dma = pltpu.SemaphoreType.DMA
    V = pltpu.VMEM
    gradient, resid, scal = pl.pallas_call(
        functools.partial(kernel, n_shot, n_gx),
        out_shape=(
            jax.ShapeDtypeStruct((CX, NY, NZ), f32),
            jax.ShapeDtypeStruct((NS, STEPS, REC), f32),
            jax.ShapeDtypeStruct((16, HALF), f32),
        ),
        in_specs=[hbm] * 9 + [smem] * 3 + [vmem] * 3,
        out_specs=(vmem, vmem, vmem),
        scratch_shapes=[
            V((2, NS, 2, CX + 2, PY, HALF), f32),
            V((2, NS, 2, CX + 2, PY, HALF), f32),
            V((NS, 2, CX + 2, PY, HALF), f32),
            V((NS, 2, CX + 2, PY, HALF), f32),
            V((NS, 2, CU, PY, HALF), f32),
            V((NS, 2, CU, PY, HALF), f32),
            V((NS, STEPS, CX, NY, NZ), f32),
            V(wide, f32),
            V(slab, f32),
            V(wide, f32),
            V(wide, f32),
            V(wide, f32),
            V(wide, f32),
            V((NS,) + slab, f32),
            V((CU * NY, REC), bf16),
            V((NZ, REC), bf16),
            V((3, 2 * REC, NZ), bf16),
            V((16, REC), f32),
            V((2, 16, REC), f32),
            V((NS * STEPS, REC), f32),
            V((2, NS * STEPS, REC), f32),
            V((2, 3, NS * STEPS, REC), f32),
            V((NS * STEPS, CU, NY, NZ), f32),
            V((CX, NY, NZ), f32),
            V((CX, NY, NZ), f32),
            V((n_shot - 1, NY, NZ), f32),
            V((2, 2, 8, HALF), f32),
            V((2, n_shot, 8, HALF), f32),
            V((2, n_gx, 8, HALF), f32),
            dma((17,)),
            dma((STEPS, NS, 2)),
            dma((STEPS, NS, 2)),
            dma((STEPS, 2)),
            dma((STEPS, 2)),
            dma((3, 2)),
            dma((3, 2)),
            dma((2, n_shot)),
            dma((2, n_shot)),
            dma((2, n_gx)),
            dma((2, n_gx)),
            dma((2, n_shot)),
            dma((2, n_shot)),
        ],
        compiler_params=pltpu.CompilerParams(
            collective_id=0,
            has_side_effects=True,
            vmem_limit_bytes=58 * 1024 * 1024,
        ),
        name="lsrtm",
    )(
        courant,
        direction,
        back_prev,
        back_now,
        scat_prev,
        scat_now,
        back_end,
        back_before_end,
        back_band,
        absorb,
        wavelet,
        grad_norm,
        jnp.transpose(src_pos, (2, 0, 1)),
        jnp.transpose(rec_pos, (2, 0, 1)),
        residual,
    )
    return pl.pallas_call(
        finish,
        out_shape=[
            jax.ShapeDtypeStruct((CX, NY, NZ), f32),
            jax.ShapeDtypeStruct((CX, NY, NZ), f32),
            jax.ShapeDtypeStruct((NS, STEPS, REC), f32),
        ],
        in_specs=[vmem] * 5,
        out_specs=[pl.BlockSpec(memory_space=pltpu.HBM)] * 3,
        scratch_shapes=[V((CX, NY, NZ), f32), V((CX, NY, NZ), f32), dma((5,))],
        compiler_params=pltpu.CompilerParams(vmem_limit_bytes=16 * 1024 * 1024),
        name="finish",
    )(scal, gradient, direction, model_image, resid)


def solution(mesh):
    field = P("shot", "gx", None, None)
    grid = P("gx", None, None)
    in_specs = (
        grid,
        P(),
        grid,
        grid,
        field,
        field,
        field,
        field,
        field,
        field,
        P("shot", None, "gx", None, None),
        P("shot", None, None),
        P("shot", None),
        P("shot", "gx", None),
        P("shot", None, "gx"),
        P(),
    )
    return jax.shard_map(
        functools.partial(per_device, mesh.shape["shot"], mesh.shape["gx"]),
        mesh=mesh,
        in_specs=in_specs,
        out_specs=(grid, grid, P("shot", None, "gx")),
        check_vma=False,
    )
```

```python
import functools

import jax
import jax.numpy as jnp
from jax import lax
from jax.experimental import pallas as pl
from jax.experimental.pallas import tpu as pltpu
from jax.sharding import PartitionSpec as P

damp_peak = 0.4
tiny = 1e-6
CX, NY, NZ = 8, 64, 256
NS, STEPS, REC, SRC = 2, 4, 128, 64
PY = 80
HU = 3
CU = CX + 2 * HU
HALF = 128
MESH = pl.DeviceIdType.MESH
f32 = jnp.float32
bf16 = jnp.bfloat16


def split2(v):
    hi = v.astype(bf16)
    lo = (v - hi.astype(f32)).astype(bf16)
    return hi, lo


def profile(pos, extent, low, high):
    gap = extent - 1 - pos
    low_f = low.astype(f32)
    high_f = high.astype(f32)
    near_low = jnp.where(pos < low, ((low - pos).astype(f32) / low_f) ** 2, 0.0)
    near_high = jnp.where(gap < high, ((high - gap).astype(f32) / high_f) ** 2, 0.0)
    return damp_peak * (near_low + near_high)


def kernel(
    n_shot,
    n_gx,
    courant_h,
    direction_h,
    back_prev_h,
    back_now_h,
    scat_prev_h,
    scat_now_h,
    back_end_h,
    back_before_h,
    band_h,
    absorb,
    wavelet,
    grad_norm,
    src_pos,
    rec_pos,
    residual,
    grad_o,
    aux_o,
    F0,
    F1,
    R0,
    R1,
    U0,
    U1,
    band,
    c0,
    dirv,
    ca,
    cb,
    cc,
    inv,
    cnt,
    rowhot,
    zt,
    zh2,
    info,
    info_n,
    tr,
    tr_n,
    amt_s,
    E,
    img_r,
    img_t,
    rs,
    ebuf,
    eslot_s,
    eslot_g,
    ld_sem,
    f_send,
    f_recv,
    r_send,
    r_recv,
    h_send,
    h_recv,
    e_send_s,
    e_recv_s,
    e_send_g,
    e_recv_g,
    g_send,
    g_recv,
):
    me_s = lax.axis_index("shot")
    me_g = lax.axis_index("gx")
    has_left = me_g > 0
    has_right = me_g < n_gx - 1
    F = (F0, F1)
    R = (R0, R1)
    U = (U0, U1)
    own = pl.ds(HU, CX)
    data = pl.ds(8, NY)
    every = slice(None)

    loads = {}
    count_l = [0]

    def load(name, src, dst):
        c = pltpu.make_async_copy(src, dst, ld_sem.at[count_l[0]])
        count_l[0] += 1
        c.start()
        loads.setdefault(name, []).append(c)

    def wait_load(name):
        for c in loads[name]:
            c.wait()

    def load_field(name, src, dst):
        for z in range(2):
            load(name, src.at[:, :, :, pl.ds(z * HALF, HALF)], dst.at[:, z, pl.ds(1, CX), data, :])

    load_field("b0", back_now_h, F0.at[0])
    load_field("s0", scat_now_h, F0.at[1])
    load_field("r0", back_before_h, R0)
    for z in range(2):
        load("c", courant_h.at[:, :, pl.ds(z * HALF, HALF)], c0.at[z, own])
    load_field("bs1", back_prev_h, F1.at[0])
    load_field("bs1", scat_prev_h, F1.at[1])
    for z in range(2):
        load("bs1", direction_h.at[:, :, pl.ds(z * HALF, HALF)], dirv.at[z])
    load_field("r1", back_end_h, R1)
    load("r1", band_h, band)

    zero8 = jnp.zeros((8, HALF), f32)
    zero64 = jnp.zeros((NY, HALF), f32)
    lead_f = [(f, s, z) for f in range(2) for s in range(NS) for z in range(2)]
    lead_r = [(s, z) for s in range(NS) for z in range(2)]
    for p in (0, CX + 1):
        for b in range(2):
            for idx in lead_f:
                F[b][idx + (p, data, every)] = zero64
            for idx in lead_r:
                R[b][idx + (p, data, every)] = zero64
    for z in range(2):
        for p in range(HU):
            c0[z, p] = zero64
            c0[z, HU + CX + p] = zero64
    for g in range(2):
        info_n[g, pl.ds(0, 8), :] = zero8
        info_n[g, pl.ds(8, 8), :] = zero8
        tr_n[g] = zero8

    bar = pltpu.get_barrier_semaphore()
    for d in range(1, n_gx):
        pl.semaphore_signal(
            bar, inc=1, device_id=(me_s, lax.rem(me_g + d, n_gx)), device_id_type=MESH
        )
    for d in range(1, n_shot):
        pl.semaphore_signal(
            bar, inc=1, device_id=(lax.rem(me_s + d, n_shot), me_g), device_id_type=MESH
        )

    rec_row = (rec_pos[0, 0:1, :] * NY + rec_pos[1, 0:1, :]).astype(f32)
    rec_z = rec_pos[2, 0:1, :].astype(f32)
    for s in range(NS):
        info[pl.ds(s * STEPS, STEPS), :] = residual[s]
    info[pl.ds(8, 1), :] = rec_row
    info[pl.ds(9, 1), :] = rec_z
    info[pl.ds(10, 6), :] = jnp.zeros((6, REC), f32)

    class Pair:
        def __init__(self, to_left, to_right, send, recv):
            self.refs = (to_left, to_right)
            self.send = send
            self.recv = recv

        def copy(self, side):
            src, dst = self.refs[side]
            return pltpu.make_async_remote_copy(
                src_ref=src,
                dst_ref=dst,
                send_sem=self.send.at[side],
                recv_sem=self.recv.at[side],
                device_id=(me_s, me_g - 1 if side == 0 else me_g + 1),
                device_id_type=MESH,
            )

        def start(self):
            @pl.when(has_left)
            def _():
                self.copy(0).start()

            @pl.when(has_right)
            def _():
                self.copy(1).start()

        def wait_recv(self):
            @pl.when(has_right)
            def _():
                self.copy(0).wait_recv()

            @pl.when(has_left)
            def _():
                self.copy(1).wait_recv()

        def wait_send(self):
            @pl.when(has_left)
            def _():
                self.copy(0).wait_send()

            @pl.when(has_right)
            def _():
                self.copy(1).wait_send()

    def face(buf, lead, p):
        return buf.at[(every,) * lead + (p, data, every)]

    def bs_faces(n, s):
        b = F[n % 2]
        return Pair(
            (b.at[:, s, :, 1, data, :], b.at[:, s, :, CX + 1, data, :]),
            (b.at[:, s, :, CX, data, :], b.at[:, s, :, 0, data, :]),
            f_send.at[n, s],
            f_recv.at[n, s],
        )

    def r_faces(n):
        b = R[n % 2]
        return Pair(
            (face(b, 2, 1), face(b, 2, CX + 1)),
            (face(b, 2, CX), face(b, 2, 0)),
            r_send.at[n],
            r_recv.at[n],
        )

    c_halo = Pair(
        (c0.at[:, pl.ds(HU, HU)], c0.at[:, pl.ds(HU + CX, HU)]),
        (c0.at[:, pl.ds(CX, HU)], c0.at[:, pl.ds(0, HU)]),
        h_send.at[0],
        h_recv.at[0],
    )
    info_halo = Pair((info, info_n.at[1]), (info, info_n.at[0]), h_send.at[1], h_recv.at[1])
    tr_halo = Pair((tr, tr_n.at[1]), (tr, tr_n.at[0]), h_send.at[2], h_recv.at[2])

    def pads(p, carry):
        for b in range(2):
            for idx in lead_f:
                F[b][idx + (p, pl.ds(0, 8), every)] = zero8
                F[b][idx + (p, pl.ds(72, 8), every)] = zero8
            for idx in lead_r:
                R[b][idx + (p, pl.ds(0, 8), every)] = zero8
                R[b][idx + (p, pl.ds(72, 8), every)] = zero8
        return carry

    lax.fori_loop(0, CX + 2, pads, 0)

    def pads_u(p, carry):
        for b in range(2):
            for idx in lead_r:
                U[b][idx + (p, pl.ds(0, 8), every)] = zero8
                U[b][idx + (p, pl.ds(72, 8), every)] = zero8
        return carry

    lax.fori_loop(0, CU, pads_u, 0)

    def to_col(row, n):
        eye = lax.broadcasted_iota(jnp.int32, (n, n), 0) == lax.broadcasted_iota(
            jnp.int32, (n, n), 1
        )
        return jnp.sum(jnp.where(eye, row, 0.0), axis=1, keepdims=True)

    first_row = ((me_g * CX - HU) * NY).astype(f32)

    def hot_rows(row, lo, n):
        rows = lax.broadcasted_iota(jnp.int32, (n, REC), 0).astype(f32) + (first_row + lo)
        rowhot[pl.ds(lo, n), :] = jnp.where(rows == row, 1.0, 0.0).astype(bf16)

    lane_z = lax.broadcasted_iota(jnp.int32, (REC, NZ), 1).astype(f32)

    def hot_z(z_row, g):
        hot = jnp.where(lane_z == to_col(z_row, REC), 1.0, 0.0).astype(bf16)
        zh2[g, pl.ds(0, REC), :] = hot
        zh2[g, pl.ds(REC, REC), :] = hot

    hot_rows(rec_row, HU * NY, CX * NY)
    hot_z(rec_z, 1)
    zt[...] = jnp.where(
        lax.broadcasted_iota(jnp.int32, (NZ, REC), 0).astype(f32) == rec_z, 1.0, 0.0
    ).astype(bf16)

    pl.semaphore_wait(bar, n_gx - 1 + n_shot - 1)
    wait_load("b0")
    wait_load("s0")
    for s in range(NS):
        bs_faces(0, s).start()
    wait_load("r0")
    r_faces(0).start()
    info_halo.start()
    wait_load("c")
    c_halo.start()

    nx = n_gx * CX
    lane = lax.broadcasted_iota(jnp.int32, (8, HALF), 1)
    sub = lax.broadcasted_iota(jnp.int32, (8, HALF), 0)
    damp_z = [profile(lane + z * HALF, NZ, absorb[4], absorb[5]) for z in range(2)]

    def coef(i, carry):
        pos_x = jnp.full((8, HALF), me_g * CX - HU + i, jnp.int32)
        damp_x = profile(pos_x, nx, absorb[0], absorb[1])
        for y in range(8):
            ys = pl.ds(y * 8, 8)
            damp_xy = damp_x + profile(sub + y * 8, NY, absorb[2], absorb[3])
            for z in range(2):
                damping = damp_xy + damp_z[z]
                c = c0[z, i, ys, :]
                iv = 1.0 / (1.0 + damping)
                inv[z, i, ys, :] = iv
                ca[z, i, ys, :] = (2.0 - 6.0 * c) * iv
                cb[z, i, ys, :] = (1.0 - damping) * iv
                cc[z, i, ys, :] = c * iv
        return carry

    lax.fori_loop(HU, HU + CX, coef, 0)

    src_hot = []
    for s in range(NS):
        s_row = ((src_pos[0, s : s + 1, :] - me_g * CX) * NY + src_pos[1, s : s + 1, :]).astype(
            f32
        )
        s_z = to_col(src_pos[2, s : s + 1, :].astype(f32), SRC)
        s_hot = jnp.where(
            lax.broadcasted_iota(jnp.int32, (SRC, NZ), 1).astype(f32) == s_z, 1.0, 0.0
        ).astype(bf16)
        src_hot.append((s_row, s_hot))

    def count(p, carry):
        rows = (lax.broadcasted_iota(jnp.int32, (NY, SRC), 0) + p * NY).astype(f32)
        for s in range(NS):
            hot = jnp.where(rows == src_hot[s][0], 1.0, 0.0).astype(bf16)
            n = jnp.dot(hot, src_hot[s][1], preferred_element_type=f32)
            for z in range(2):
                cnt[s, z, p] = n[:, z * HALF : (z + 1) * HALF] * inv[z, HU + p]
        return carry

    lax.fori_loop(0, CX, count, 0, unroll=2)

    first = lane == 0
    last = lane == HALF - 1

    def neighbours(ref, lead, p, y8):
        ys = pl.ds(8 + y8, 8)
        mid = [ref[lead + (z, p, ys, every)] for z in range(2)]
        right = [pltpu.roll(m, 1, 1) for m in mid]
        left = [pltpu.roll(m, HALF - 1, 1) for m in mid]
        low = [jnp.where(first, 0.0, right[0]), jnp.where(first, right[0], right[1])]
        high = [jnp.where(last, left[1], left[0]), jnp.where(last, 0.0, left[1])]
        sums = []
        for z in range(2):
            t = ref[lead + (z, p + 1, ys, every)] + ref[lead + (z, p - 1, ys, every)]
            t = t + (
                ref[lead + (z, p, pl.ds(y8 + 9, 8), every)]
                + ref[lead + (z, p, pl.ds(y8 + 7, 8), every)]
            )
            sums.append(t + (low[z] + high[z]))
        return mid, sums

    def step_bs(n, p, shots):
        now, nxt = F[n % 2], F[(n + 1) % 2]
        q = p - 1
        i = q + HU

        def chunk(j, carry):
            y8 = pl.multiple_of(j * 8, 8)
            ys = pl.ds(y8, 8)
            ysp = pl.ds(pl.multiple_of(y8 + 8, 8), 8)
            a = [ca[z, i, ys, :] for z in range(2)]
            b = [cb[z, i, ys, :] for z in range(2)]
            c = [cc[z, i, ys, :] for z in range(2)]
            di = [dirv[z, q, ys, :] for z in range(2)]
            for s in shots:
                w = wavelet[s, n]
                mid, sums = neighbours(now, (0, s), p, y8)
                acc = []
                for z in range(2):
                    old = nxt[0, s, z, p, ysp, :]
                    new = (
                        a[z] * mid[z]
                        - b[z] * old
                        + c[z] * sums[z]
                        + w * cnt[s, z, q, ys, :]
                    )
                    nxt[0, s, z, p, ysp, :] = new
                    acc.append((new - mid[z]) - (mid[z] - old))
                mid, sums = neighbours(now, (1, s), p, y8)
                for z in range(2):
                    old = nxt[1, s, z, p, ysp, :]
                    nxt[1, s, z, p, ysp, :] = (
                        a[z] * mid[z] - b[z] * old + c[z] * (sums[z] - di[z] * acc[z])
                    )
            return carry

        lax.fori_loop(0, 8, chunk, 0, unroll=8)

    def step_r(n, p):
        now, nxt = R[n % 2], R[(n + 1) % 2]
        q = p - 1
        i = q + HU
        m = STEPS - 1 - n

        def chunk(j, carry):
            y8 = pl.multiple_of(j * 8, 8)
            ys = pl.ds(y8, 8)
            ysp = pl.ds(pl.multiple_of(y8 + 8, 8), 8)
            a = [ca[z, i, ys, :] for z in range(2)]
            c = [cc[z, i, ys, :] for z in range(2)]
            layer = [cb[z, i, ys, :] < 1.0 for z in range(2)]
            for s in range(NS):
                w = wavelet[s, m]
                mid, sums = neighbours(now, (s,), p, y8)
                for z in range(2):
                    zs = pl.ds(z * HALF, HALF)
                    old = nxt[s, z, p, ysp, :]
                    new = a[z] * mid[z] - old + c[z] * sums[z] + w * cnt[s, z, q, ys, :]
                    new = jnp.where(layer[z], band[s, m, q, ys, zs], new)
                    nxt[s, z, p, ysp, :] = new
                    band[s, m, q, ys, zs] = (new - mid[z]) - (mid[z] - old)
            return carry

        lax.fori_loop(0, 8, chunk, 0, unroll=8)

    def gather(n):
        ref = F[(n + 1) % 2]
        zero = jnp.zeros((NY, REC), f32)

        def one(p, carry):
            hot = rowhot[pl.ds(pl.multiple_of((p + HU) * NY, NY), NY), :].astype(f32)
            parts = []
            for s in range(NS):
                v = jnp.concatenate([ref[1, s, z, p + 1, data, :] for z in range(2)], axis=1)
                parts.extend(split2(v))
            g = jnp.dot(jnp.concatenate(parts, axis=0), zt[...], preferred_element_type=f32)
            return tuple(
                carry[s] + hot * (g[2 * s * NY : (2 * s + 1) * NY] + g[(2 * s + 1) * NY : (2 * s + 2) * NY])
                for s in range(NS)
            )

        got = lax.fori_loop(0, CX, one, (zero, zero), unroll=8)
        for s in range(NS):
            tr[pl.ds(s * STEPS + n, 1), :] = jnp.sum(got[s], axis=0, keepdims=True)

    def inject(kind, lo, hi):
        def plane(i, carry):
            g = (i + CX - HU) // CX
            hot = rowhot[pl.ds(pl.multiple_of(i * NY, NY), NY), :].astype(f32)
            for s in range(NS):
                parts = []
                for n in range(STEPS):
                    v = amt_s[kind, g, pl.ds(s * STEPS + n, 1), :]
                    v_hi = v.astype(bf16).astype(f32)
                    parts.append(
                        jnp.concatenate(
                            [(hot * v_hi).astype(bf16), (hot * (v - v_hi)).astype(bf16)], axis=1
                        )
                    )
                e = jnp.dot(jnp.concatenate(parts, axis=0), zh2[g], preferred_element_type=f32)
                for n in range(STEPS):
                    E[s * STEPS + n, i] = e[n * NY : (n + 1) * NY]
            return carry

        lax.fori_loop(lo, hi, plane, 0)

    def level(m, img):
        now, nxt = U[(m + 1) % 2], U[m % 2]
        n = STEPS - 1 - m

        def plane(image, i, carry):
            q = i - HU

            def chunk(j, inner):
                y8 = pl.multiple_of(j * 8, 8)
                ys = pl.ds(y8, 8)
                ysp = pl.ds(pl.multiple_of(y8 + 8, 8), 8)
                pic = [None, None]
                for s in range(NS):
                    if m > 0:
                        mid, sums = neighbours(now, (s,), i, y8)
                    for z in range(2):
                        zs = pl.ds(z * HALF, HALF)
                        u = inv[z, i, ys, :] * E[s * STEPS + n, i, ys, zs]
                        if m > 0:
                            u = u + (ca[z, i, ys, :] * mid[z] + cc[z, i, ys, :] * sums[z])
                        if m > 1:
                            u = u - cb[z, i, ys, :] * nxt[s, z, i, ysp, :]
                        if m < STEPS - 1:
                            nxt[s, z, i, ysp, :] = u
                        if image:
                            part = band[s, n, q, ys, pl.ds(z * HALF, HALF)] * u
                            pic[z] = part if s == 0 else pic[z] + part
                if image:
                    for z in range(2):
                        zs = pl.ds(z * HALF, HALF)
                        old = 0.0 if m == 0 else img[q, ys, zs]
                        img[q, ys, zs] = old + pic[z]
                return inner

            lax.fori_loop(0, 8, chunk, 0, unroll=8)
            return carry

        if m < STEPS - 1:
            lax.fori_loop(m, HU, functools.partial(plane, False), 0)
            lax.fori_loop(HU + CX, CU - m, functools.partial(plane, False), 0)
        lax.fori_loop(HU, HU + CX, functools.partial(plane, True), 0, unroll=2)

    def edge_bs(n, s):
        def one(k, carry):
            step_bs(n, 1 + (CX - 1) * k, (s,))
            return carry

        lax.fori_loop(0, 2, one, 0, unroll=2)

    def edge_r(n):
        def one(k, carry):
            step_r(n, 1 + (CX - 1) * k)
            return carry

        lax.fori_loop(0, 2, one, 0)

    def inner_bs(n, shots):
        def one(p, carry):
            step_bs(n, p, shots)
            return carry

        lax.fori_loop(2, CX, one, 0, unroll=2)

    def inner_r(n):
        def one(p, carry):
            step_r(n, p)
            return carry

        lax.fori_loop(2, CX, one, 0, unroll=2)

    for n in range(STEPS):
        if n == 0:
            wait_load("bs1")
            inner_bs(n, range(NS))
            wait_load("r1")
            inner_r(n)
        for s in range(NS):
            bs_faces(n, s).wait_recv()
            if n > 0:
                bs_faces(n - 1, s).wait_send()
            edge_bs(n, s)
            if n < STEPS - 1:
                bs_faces(n + 1, s).start()
            if n > 0:
                inner_bs(n, (s,))
        r_faces(n).wait_recv()
        if n > 0:
            r_faces(n - 1).wait_send()
        edge_r(n)
        if n < STEPS - 1:
            r_faces(n + 1).start()
        if n > 0:
            inner_r(n)
        gather(n)
        if n == 0:
            info_halo.wait_recv()
            c_halo.wait_recv()
            for g, lo in ((0, 0), (1, (HU + CX) * NY)):
                hot_rows(info_n[g, pl.ds(8, 1), :], lo, HU * NY)
                hot_z(info_n[g, pl.ds(9, 1), :], 2 * g)
            lax.fori_loop(0, HU, coef, 0)
            lax.fori_loop(HU + CX, CU, coef, 0)
            amt_s[0, 0] = info_n[0, pl.ds(0, 8), :]
            amt_s[0, 1] = info[pl.ds(0, 8), :]
            amt_s[0, 2] = info_n[1, pl.ds(0, 8), :]
            inject(0, 0, CU)
        level(n, img_r)
    for s in range(NS):
        bs_faces(STEPS - 1, s).wait_send()
    r_faces(STEPS - 1).wait_send()
    info_halo.wait_send()
    c_halo.wait_send()

    def to_slabs(r):
        return [
            pltpu.make_async_remote_copy(
                src_ref=ebuf.at[r, 0],
                dst_ref=eslot_g.at[r, me_g],
                send_sem=e_send_g.at[r, d],
                recv_sem=e_recv_g.at[r, d],
                device_id=(me_s, lax.rem(me_g + d, n_gx)),
                device_id_type=MESH,
            )
            for d in range(1, n_gx)
        ]

    def to_shots(r):
        return [
            pltpu.make_async_remote_copy(
                src_ref=ebuf.at[r, 1],
                dst_ref=eslot_s.at[r, me_s],
                send_sem=e_send_s.at[r, d],
                recv_sem=e_recv_s.at[r, d],
                device_id=(lax.rem(me_s + d, n_shot), me_g),
                device_id_type=MESH,
            )
            for d in range(1, n_shot)
        ]

    def sum_start(value, r):
        ebuf[r, 0] = value
        eslot_g[r, me_g] = value
        for c in to_slabs(r):
            c.start()

    def sum_middle(r):
        for c in to_slabs(r):
            c.wait_recv()
        total = eslot_g[r, 0]
        for d in range(1, n_gx):
            total = total + eslot_g[r, d]
        ebuf[r, 1] = total
        eslot_s[r, me_s] = total
        for c in to_shots(r):
            c.start()

    def sum_end(r):
        for c in to_shots(r):
            c.wait_recv()
        total = eslot_s[r, 0]
        for d in range(1, n_shot):
            total = total + eslot_s[r, d]
        return jnp.sum(total)

    t = tr[...]
    tr_halo.start()
    sum_start(t * t, 0)
    amt_s[1, 1] = t
    inject(1, HU, HU + CX)
    tr_halo.wait_recv()
    amt_s[1, 0] = tr_n[0]
    amt_s[1, 2] = tr_n[1]
    inject(1, 0, HU)
    inject(1, HU + CX, CU)
    level(0, img_t)
    sum_middle(0)
    for m in range(1, STEPS - 1):
        level(m, img_t)
    energy = sum_end(0)
    gn = jnp.full((8, HALF), grad_norm[0], f32)
    step = gn / (jnp.full((8, HALF), energy, f32) + tiny)
    for s in range(NS):
        aux_o[pl.ds(s * STEPS, STEPS), :] = (
            residual[s] - step[0:STEPS] * t[s * STEPS : (s + 1) * STEPS]
        )

    def to_sum(d):
        to = lax.rem(me_s + d, n_shot)
        return pltpu.make_async_remote_copy(
            src_ref=img_r.at[to],
            dst_ref=rs.at[d - 1],
            send_sem=g_send.at[0, d],
            recv_sem=g_recv.at[0, d],
            device_id=(to, me_g),
            device_id_type=MESH,
        )

    m_last = STEPS - 1
    now_u, old_u = U[(m_last + 1) % 2], U[m_last % 2]

    def gradient_plane(d, carry):
        q = lax.rem(me_s + d, n_shot)
        i = q + HU

        def chunk(j, inner):
            y8 = pl.multiple_of(j * 8, 8)
            ys = pl.ds(y8, 8)
            ysp = pl.ds(pl.multiple_of(y8 + 8, 8), 8)
            pic = [img_t[q, ys, pl.ds(z * HALF, HALF)] for z in range(2)]
            for s in range(NS):
                mid, sums = neighbours(now_u, (s,), i, y8)
                for z in range(2):
                    zs = pl.ds(z * HALF, HALF)
                    u = inv[z, i, ys, :] * E[s * STEPS, i, ys, zs]
                    u = u + (ca[z, i, ys, :] * mid[z] + cc[z, i, ys, :] * sums[z])
                    u = u - cb[z, i, ys, :] * old_u[s, z, i, ysp, :]
                    pic[z] = pic[z] + band[s, 0, q, ys, zs] * u
            for z in range(2):
                zs = pl.ds(z * HALF, HALF)
                img_r[q, ys, zs] = c0[z, i, ys, :] * (step * pic[z] - img_r[q, ys, zs])
            return inner

        lax.fori_loop(0, 8, chunk, 0, unroll=8)

        @pl.when(d < n_shot)
        def _():
            to_sum(d).start()

        return carry

    lax.fori_loop(1, n_shot + 1, gradient_plane, 0)
    for d in range(1, n_shot):
        to_sum(d).wait_recv()

    def add(i, carry):
        ys = pl.ds(pl.multiple_of(i * 8, 8), 8)
        g = img_r[me_s, ys, :]
        for d in range(1, n_shot):
            g = g + rs[d - 1, ys, :]
        grad_o[me_s, ys, :] = g
        g = g * g
        return carry + (g[:, :HALF] + g[:, HALF:])

    part = lax.fori_loop(0, 8, add, jnp.zeros((8, HALF), f32), unroll=8)
    sum_start(part, 1)
    def spread(d):
        return pltpu.make_async_remote_copy(
            src_ref=grad_o.at[me_s],
            dst_ref=grad_o.at[me_s],
            send_sem=g_send.at[1, d],
            recv_sem=g_recv.at[1, d],
            device_id=(lax.rem(me_s + d, n_shot), me_g),
            device_id_type=MESH,
        )

    for d in range(1, n_shot, 2):
        spread(d).start()
    sum_middle(1)
    for d in range(2, n_shot, 2):
        spread(d).start()
    grad_energy = sum_end(1)
    ratio = jnp.full((8, HALF), grad_energy, f32) / gn
    aux_o[pl.ds(8, 8), :] = step
    aux_o[pl.ds(16, 8), :] = ratio
    for d in range(1, n_shot):
        came = lax.rem(me_s + n_shot - d, n_shot)
        pltpu.make_async_remote_copy(
            src_ref=grad_o.at[came],
            dst_ref=grad_o.at[came],
            send_sem=g_send.at[1, d],
            recv_sem=g_recv.at[1, d],
            device_id=(came, me_g),
            device_id_type=MESH,
        ).wait_recv()
    tr_halo.wait_send()
    for r in range(2):
        for c in to_shots(r) + to_slabs(r):
            c.wait_send()
    for d in range(1, n_shot):
        to_sum(d).wait_send()
        spread(d).wait_send()


def finish(
    aux_h, gradient_h, direction_h, model_h, image_o, dir_o, resid_o,
    aux, gradient, direction, image, resid, sem,
):
    half = CX // 2
    first = pltpu.make_async_copy(aux_h, aux, sem.at[0])
    first.start()
    come = []
    for k in range(2):
        ps = pl.ds(k * half, half)
        for b, (src, dst) in enumerate(
            ((gradient_h, gradient), (direction_h, direction), (model_h, image))
        ):
            c = pltpu.make_async_copy(src.at[ps], dst.at[ps], sem.at[1 + 3 * k + b])
            c.start()
            come.append(c)
    first.wait()
    step = aux[8:9, 0:1]
    ratio = aux[16:17, 0:1]
    for s in range(NS):
        resid[s] = aux[s * STEPS : (s + 1) * STEPS, :]
    gone = [pltpu.make_async_copy(resid, resid_o, sem.at[7])]
    gone[0].start()
    for k in range(2):
        ps = pl.ds(k * half, half)
        for c in come[3 * k : 3 * k + 3]:
            c.wait()

        def plane(p, carry):
            d = direction[p]
            image[p] = image[p] + step * d
            gradient[p] = gradient[p] + ratio * d
            return carry

        lax.fori_loop(k * half, (k + 1) * half, plane, 0)
        for b, (src, dst) in enumerate(((image, image_o), (gradient, dir_o))):
            c = pltpu.make_async_copy(src.at[ps], dst.at[ps], sem.at[8 + 2 * k + b])
            c.start()
            gone.append(c)
    for c in gone:
        c.wait()


def per_device(
    n_shot,
    n_gx,
    courant,
    absorb,
    model_image,
    direction,
    back_prev,
    back_now,
    scat_prev,
    scat_now,
    back_end,
    back_before_end,
    back_band,
    src_pos,
    wavelet,
    rec_pos,
    residual,
    grad_norm,
):
    hbm = pl.BlockSpec(memory_space=pl.ANY)
    vmem = pl.BlockSpec(memory_space=pltpu.VMEM)
    smem = pl.BlockSpec(memory_space=pltpu.SMEM)
    slab = (2, CX, NY, HALF)
    wide = (2, CU, NY, HALF)
    dma = pltpu.SemaphoreType.DMA
    V = pltpu.VMEM
    gradient, aux = pl.pallas_call(
        functools.partial(kernel, n_shot, n_gx),
        out_shape=(
            jax.ShapeDtypeStruct((CX, NY, NZ), f32),
            jax.ShapeDtypeStruct((24, HALF), f32),
        ),
        in_specs=[hbm] * 9 + [smem] * 3 + [vmem] * 3,
        out_specs=(vmem, vmem),
        scratch_shapes=[
            V((2, NS, 2, CX + 2, PY, HALF), f32),
            V((2, NS, 2, CX + 2, PY, HALF), f32),
            V((NS, 2, CX + 2, PY, HALF), f32),
            V((NS, 2, CX + 2, PY, HALF), f32),
            V((NS, 2, CU, PY, HALF), f32),
            V((NS, 2, CU, PY, HALF), f32),
            V((NS, STEPS, CX, NY, NZ), f32),
            V(wide, f32),
            V(slab, f32),
            V(wide, f32),
            V(wide, f32),
            V(wide, f32),
            V(wide, f32),
            V((NS,) + slab, f32),
            V((CU * NY, REC), bf16),
            V((NZ, REC), bf16),
            V((3, 2 * REC, NZ), bf16),
            V((16, REC), f32),
            V((2, 16, REC), f32),
            V((NS * STEPS, REC), f32),
            V((2, NS * STEPS, REC), f32),
            V((2, 3, NS * STEPS, REC), f32),
            V((NS * STEPS, CU, NY, NZ), f32),
            V((CX, NY, NZ), f32),
            V((CX, NY, NZ), f32),
            V((n_shot - 1, NY, NZ), f32),
            V((2, 2, 8, HALF), f32),
            V((2, n_shot, 8, HALF), f32),
            V((2, n_gx, 8, HALF), f32),
            dma((17,)),
            dma((STEPS, NS, 2)),
            dma((STEPS, NS, 2)),
            dma((STEPS, 2)),
            dma((STEPS, 2)),
            dma((3, 2)),
            dma((3, 2)),
            dma((2, n_shot)),
            dma((2, n_shot)),
            dma((2, n_gx)),
            dma((2, n_gx)),
            dma((2, n_shot)),
            dma((2, n_shot)),
        ],
        compiler_params=pltpu.CompilerParams(
            collective_id=0,
            has_side_effects=True,
            vmem_limit_bytes=58 * 1024 * 1024,
        ),
        name="lsrtm",
    )(
        courant,
        direction,
        back_prev,
        back_now,
        scat_prev,
        scat_now,
        back_end,
        back_before_end,
        back_band,
        absorb,
        wavelet,
        grad_norm,
        jnp.transpose(src_pos, (2, 0, 1)),
        jnp.transpose(rec_pos, (2, 0, 1)),
        residual,
    )
    return pl.pallas_call(
        finish,
        out_shape=[
            jax.ShapeDtypeStruct((CX, NY, NZ), f32),
            jax.ShapeDtypeStruct((CX, NY, NZ), f32),
            jax.ShapeDtypeStruct((NS, STEPS, REC), f32),
        ],
        in_specs=[hbm] * 4,
        out_specs=[pl.BlockSpec(memory_space=pltpu.HBM)] * 3,
        scratch_shapes=[
            V((24, HALF), f32),
            V((CX, NY, NZ), f32),
            V((CX, NY, NZ), f32),
            V((CX, NY, NZ), f32),
            V((NS, STEPS, REC), f32),
            dma((12,)),
        ],
        compiler_params=pltpu.CompilerParams(vmem_limit_bytes=62 * 1024 * 1024),
        name="finish",
    )(aux, gradient, direction, model_image)


def solution(mesh):
    field = P("shot", "gx", None, None)
    grid = P("gx", None, None)
    in_specs = (
        grid,
        P(),
        grid,
        grid,
        field,
        field,
        field,
        field,
        field,
        field,
        P("shot", None, "gx", None, None),
        P("shot", None, None),
        P("shot", None),
        P("shot", "gx", None),
        P("shot", None, "gx"),
        P(),
    )
    return jax.shard_map(
        functools.partial(per_device, mesh.shape["shot"], mesh.shape["gx"]),
        mesh=mesh,
        in_specs=in_specs,
        out_specs=(grid, grid, P("shot", None, "gx")),
        check_vma=False,
    )
```

```python
import functools

import jax
import jax.numpy as jnp
from jax import lax
from jax.experimental import pallas as pl
from jax.experimental.pallas import tpu as pltpu
from jax.sharding import PartitionSpec as P

damp_peak = 0.4
tiny = 1e-6
CX, NY, NZ = 8, 64, 256
NS, STEPS, REC, SRC = 2, 4, 128, 64
PY = 80
HU = 3
CU = CX + 2 * HU
HALF = 128
MESH = pl.DeviceIdType.MESH
f32 = jnp.float32
bf16 = jnp.bfloat16


def split2(v):
    hi = v.astype(bf16)
    lo = (v - hi.astype(f32)).astype(bf16)
    return hi, lo


def profile(pos, extent, low, high):
    gap = extent - 1 - pos
    low_f = low.astype(f32)
    high_f = high.astype(f32)
    near_low = jnp.where(pos < low, ((low - pos).astype(f32) / low_f) ** 2, 0.0)
    near_high = jnp.where(gap < high, ((high - gap).astype(f32) / high_f) ** 2, 0.0)
    return damp_peak * (near_low + near_high)


def kernel(
    n_shot,
    n_gx,
    courant_h,
    direction_h,
    back_prev_h,
    back_now_h,
    scat_prev_h,
    scat_now_h,
    back_end_h,
    back_before_h,
    band_h,
    absorb,
    wavelet,
    grad_norm,
    src_pos,
    rec_pos,
    residual,
    grad_o,
    aux_o,
    F0,
    F1,
    R0,
    R1,
    U0,
    U1,
    band,
    c0,
    dirv,
    ca,
    cb,
    cc,
    inv,
    cnt,
    rowhot,
    zt,
    zh2,
    info,
    info_n,
    tr,
    tr_n,
    amt_s,
    E,
    img_r,
    img_t,
    rs,
    ebuf,
    eslot_s,
    eslot_g,
    ld_sem,
    f_send,
    f_recv,
    r_send,
    r_recv,
    h_send,
    h_recv,
    e_send_s,
    e_recv_s,
    e_send_g,
    e_recv_g,
    g_send,
    g_recv,
):
    me_s = lax.axis_index("shot")
    me_g = lax.axis_index("gx")
    has_left = me_g > 0
    has_right = me_g < n_gx - 1
    F = (F0, F1)
    R = (R0, R1)
    U = (U0, U1)
    own = pl.ds(HU, CX)
    data = pl.ds(8, NY)
    every = slice(None)

    loads = {}
    count_l = [0]

    def load(name, src, dst):
        c = pltpu.make_async_copy(src, dst, ld_sem.at[count_l[0]])
        count_l[0] += 1
        c.start()
        loads.setdefault(name, []).append(c)

    def wait_load(name):
        for c in loads[name]:
            c.wait()

    def load_field(name, src, dst):
        for z in range(2):
            load(name, src.at[:, :, :, pl.ds(z * HALF, HALF)], dst.at[:, z, pl.ds(1, CX), data, :])

    load_field("b0", back_now_h, F0.at[0])
    load_field("s0", scat_now_h, F0.at[1])
    load_field("r0", back_before_h, R0)
    for z in range(2):
        load("c", courant_h.at[:, :, pl.ds(z * HALF, HALF)], c0.at[z, own])
    load_field("bs1", back_prev_h, F1.at[0])
    load_field("bs1", scat_prev_h, F1.at[1])
    for z in range(2):
        load("bs1", direction_h.at[:, :, pl.ds(z * HALF, HALF)], dirv.at[z])
    load_field("r1", back_end_h, R1)
    load("r1", band_h, band)

    zero8 = jnp.zeros((8, HALF), f32)
    zero64 = jnp.zeros((NY, HALF), f32)
    lead_f = [(f, s, z) for f in range(2) for s in range(NS) for z in range(2)]
    lead_r = [(s, z) for s in range(NS) for z in range(2)]
    for p in (0, CX + 1):
        for b in range(2):
            for idx in lead_f:
                F[b][idx + (p, data, every)] = zero64
            for idx in lead_r:
                R[b][idx + (p, data, every)] = zero64
    for z in range(2):
        for p in range(HU):
            c0[z, p] = zero64
            c0[z, HU + CX + p] = zero64
    for g in range(2):
        info_n[g, pl.ds(0, 8), :] = zero8
        info_n[g, pl.ds(8, 8), :] = zero8
        tr_n[g] = zero8

    bar = pltpu.get_barrier_semaphore()
    for d in range(1, n_gx):
        pl.semaphore_signal(
            bar, inc=1, device_id=(me_s, lax.rem(me_g + d, n_gx)), device_id_type=MESH
        )
    for d in range(1, n_shot):
        pl.semaphore_signal(
            bar, inc=1, device_id=(lax.rem(me_s + d, n_shot), me_g), device_id_type=MESH
        )

    rec_row = (rec_pos[0, 0:1, :] * NY + rec_pos[1, 0:1, :]).astype(f32)
    rec_z = rec_pos[2, 0:1, :].astype(f32)
    for s in range(NS):
        info[pl.ds(s * STEPS, STEPS), :] = residual[s]
    info[pl.ds(8, 1), :] = rec_row
    info[pl.ds(9, 1), :] = rec_z
    info[pl.ds(10, 6), :] = jnp.zeros((6, REC), f32)

    class Pair:
        def __init__(self, to_left, to_right, send, recv):
            self.refs = (to_left, to_right)
            self.send = send
            self.recv = recv

        def copy(self, side):
            src, dst = self.refs[side]
            return pltpu.make_async_remote_copy(
                src_ref=src,
                dst_ref=dst,
                send_sem=self.send.at[side],
                recv_sem=self.recv.at[side],
                device_id=(me_s, me_g - 1 if side == 0 else me_g + 1),
                device_id_type=MESH,
            )

        def start(self):
            @pl.when(has_left)
            def _():
                self.copy(0).start()

            @pl.when(has_right)
            def _():
                self.copy(1).start()

        def wait_recv(self):
            @pl.when(has_right)
            def _():
                self.copy(0).wait_recv()

            @pl.when(has_left)
            def _():
                self.copy(1).wait_recv()

        def wait_send(self):
            @pl.when(has_left)
            def _():
                self.copy(0).wait_send()

            @pl.when(has_right)
            def _():
                self.copy(1).wait_send()

    def face(buf, lead, p):
        return buf.at[(every,) * lead + (p, data, every)]

    def bs_faces(n, s):
        b = F[n % 2]
        return Pair(
            (b.at[:, s, :, 1, data, :], b.at[:, s, :, CX + 1, data, :]),
            (b.at[:, s, :, CX, data, :], b.at[:, s, :, 0, data, :]),
            f_send.at[n, s],
            f_recv.at[n, s],
        )

    def r_faces(n):
        b = R[n % 2]
        return Pair(
            (face(b, 2, 1), face(b, 2, CX + 1)),
            (face(b, 2, CX), face(b, 2, 0)),
            r_send.at[n],
            r_recv.at[n],
        )

    c_halo = Pair(
        (c0.at[:, pl.ds(HU, HU)], c0.at[:, pl.ds(HU + CX, HU)]),
        (c0.at[:, pl.ds(CX, HU)], c0.at[:, pl.ds(0, HU)]),
        h_send.at[0],
        h_recv.at[0],
    )
    info_halo = Pair((info, info_n.at[1]), (info, info_n.at[0]), h_send.at[1], h_recv.at[1])
    tr_halo = Pair((tr, tr_n.at[1]), (tr, tr_n.at[0]), h_send.at[2], h_recv.at[2])

    def pads(p, carry):
        for b in range(2):
            for idx in lead_f:
                F[b][idx + (p, pl.ds(0, 8), every)] = zero8
                F[b][idx + (p, pl.ds(72, 8), every)] = zero8
            for idx in lead_r:
                R[b][idx + (p, pl.ds(0, 8), every)] = zero8
                R[b][idx + (p, pl.ds(72, 8), every)] = zero8
        return carry

    lax.fori_loop(0, CX + 2, pads, 0)

    def pads_u(p, carry):
        for b in range(2):
            for idx in lead_r:
                U[b][idx + (p, pl.ds(0, 8), every)] = zero8
                U[b][idx + (p, pl.ds(72, 8), every)] = zero8
        return carry

    lax.fori_loop(0, CU, pads_u, 0)

    def to_col(row, n):
        eye = lax.broadcasted_iota(jnp.int32, (n, n), 0) == lax.broadcasted_iota(
            jnp.int32, (n, n), 1
        )
        return jnp.sum(jnp.where(eye, row, 0.0), axis=1, keepdims=True)

    first_row = ((me_g * CX - HU) * NY).astype(f32)

    def hot_rows(row, lo, n):
        rows = lax.broadcasted_iota(jnp.int32, (n, REC), 0).astype(f32) + (first_row + lo)
        rowhot[pl.ds(lo, n), :] = jnp.where(rows == row, 1.0, 0.0).astype(bf16)

    lane_z = lax.broadcasted_iota(jnp.int32, (REC, NZ), 1).astype(f32)

    def hot_z(z_row, g):
        hot = jnp.where(lane_z == to_col(z_row, REC), 1.0, 0.0).astype(bf16)
        zh2[g, pl.ds(0, REC), :] = hot
        zh2[g, pl.ds(REC, REC), :] = hot

    hot_rows(rec_row, HU * NY, CX * NY)
    hot_z(rec_z, 1)
    zt[...] = jnp.where(
        lax.broadcasted_iota(jnp.int32, (NZ, REC), 0).astype(f32) == rec_z, 1.0, 0.0
    ).astype(bf16)

    pl.semaphore_wait(bar, n_gx - 1 + n_shot - 1)
    wait_load("b0")
    wait_load("s0")
    for s in range(NS):
        bs_faces(0, s).start()
    wait_load("r0")
    r_faces(0).start()
    info_halo.start()
    wait_load("c")
    c_halo.start()

    nx = n_gx * CX
    lane = lax.broadcasted_iota(jnp.int32, (8, HALF), 1)
    sub = lax.broadcasted_iota(jnp.int32, (8, HALF), 0)
    damp_z = [profile(lane + z * HALF, NZ, absorb[4], absorb[5]) for z in range(2)]

    def coef(i, carry):
        pos_x = jnp.full((8, HALF), me_g * CX - HU + i, jnp.int32)
        damp_x = profile(pos_x, nx, absorb[0], absorb[1])
        for y in range(8):
            ys = pl.ds(y * 8, 8)
            damp_xy = damp_x + profile(sub + y * 8, NY, absorb[2], absorb[3])
            for z in range(2):
                damping = damp_xy + damp_z[z]
                c = c0[z, i, ys, :]
                iv = 1.0 / (1.0 + damping)
                inv[z, i, ys, :] = iv
                ca[z, i, ys, :] = (2.0 - 6.0 * c) * iv
                cb[z, i, ys, :] = (1.0 - damping) * iv
                cc[z, i, ys, :] = c * iv
        return carry

    lax.fori_loop(HU, HU + CX, coef, 0)

    src_hot = []
    for s in range(NS):
        s_row = ((src_pos[0, s : s + 1, :] - me_g * CX) * NY + src_pos[1, s : s + 1, :]).astype(
            f32
        )
        s_z = to_col(src_pos[2, s : s + 1, :].astype(f32), SRC)
        s_hot = jnp.where(
            lax.broadcasted_iota(jnp.int32, (SRC, NZ), 1).astype(f32) == s_z, 1.0, 0.0
        ).astype(bf16)
        src_hot.append((s_row, s_hot))

    def count(p, carry):
        rows = (lax.broadcasted_iota(jnp.int32, (NY, SRC), 0) + p * NY).astype(f32)
        for s in range(NS):
            hot = jnp.where(rows == src_hot[s][0], 1.0, 0.0).astype(bf16)
            n = jnp.dot(hot, src_hot[s][1], preferred_element_type=f32)
            for z in range(2):
                cnt[s, z, p] = n[:, z * HALF : (z + 1) * HALF] * inv[z, HU + p]
        return carry

    lax.fori_loop(0, CX, count, 0, unroll=2)

    first = lane == 0
    last = lane == HALF - 1

    def neighbours(ref, lead, p, y8):
        ys = pl.ds(8 + y8, 8)
        mid = [ref[lead + (z, p, ys, every)] for z in range(2)]
        right = [pltpu.roll(m, 1, 1) for m in mid]
        left = [pltpu.roll(m, HALF - 1, 1) for m in mid]
        low = [jnp.where(first, 0.0, right[0]), jnp.where(first, right[0], right[1])]
        high = [jnp.where(last, left[1], left[0]), jnp.where(last, 0.0, left[1])]
        sums = []
        for z in range(2):
            t = ref[lead + (z, p + 1, ys, every)] + ref[lead + (z, p - 1, ys, every)]
            t = t + (
                ref[lead + (z, p, pl.ds(y8 + 9, 8), every)]
                + ref[lead + (z, p, pl.ds(y8 + 7, 8), every)]
            )
            sums.append(t + (low[z] + high[z]))
        return mid, sums

    def step_bs(n, p, shots):
        now, nxt = F[n % 2], F[(n + 1) % 2]
        q = p - 1
        i = q + HU

        def chunk(j, carry):
            y8 = pl.multiple_of(j * 8, 8)
            ys = pl.ds(y8, 8)
            ysp = pl.ds(pl.multiple_of(y8 + 8, 8), 8)
            a = [ca[z, i, ys, :] for z in range(2)]
            b = [cb[z, i, ys, :] for z in range(2)]
            c = [cc[z, i, ys, :] for z in range(2)]
            di = [dirv[z, q, ys, :] for z in range(2)]
            for s in shots:
                w = wavelet[s, n]
                mid, sums = neighbours(now, (0, s), p, y8)
                acc = []
                for z in range(2):
                    old = nxt[0, s, z, p, ysp, :]
                    new = (
                        a[z] * mid[z]
                        - b[z] * old
                        + c[z] * sums[z]
                        + w * cnt[s, z, q, ys, :]
                    )
                    nxt[0, s, z, p, ysp, :] = new
                    acc.append((new - mid[z]) - (mid[z] - old))
                mid, sums = neighbours(now, (1, s), p, y8)
                for z in range(2):
                    old = nxt[1, s, z, p, ysp, :]
                    nxt[1, s, z, p, ysp, :] = (
                        a[z] * mid[z] - b[z] * old + c[z] * (sums[z] - di[z] * acc[z])
                    )
            return carry

        lax.fori_loop(0, 8, chunk, 0, unroll=8)

    def step_r(n, p):
        now, nxt = R[n % 2], R[(n + 1) % 2]
        q = p - 1
        i = q + HU
        m = STEPS - 1 - n

        def chunk(j, carry):
            y8 = pl.multiple_of(j * 8, 8)
            ys = pl.ds(y8, 8)
            ysp = pl.ds(pl.multiple_of(y8 + 8, 8), 8)
            a = [ca[z, i, ys, :] for z in range(2)]
            c = [cc[z, i, ys, :] for z in range(2)]
            layer = [cb[z, i, ys, :] < 1.0 for z in range(2)]
            for s in range(NS):
                w = wavelet[s, m]
                mid, sums = neighbours(now, (s,), p, y8)
                for z in range(2):
                    zs = pl.ds(z * HALF, HALF)
                    old = nxt[s, z, p, ysp, :]
                    new = a[z] * mid[z] - old + c[z] * sums[z] + w * cnt[s, z, q, ys, :]
                    new = jnp.where(layer[z], band[s, m, q, ys, zs], new)
                    nxt[s, z, p, ysp, :] = new
                    band[s, m, q, ys, zs] = (new - mid[z]) - (mid[z] - old)
            return carry

        lax.fori_loop(0, 8, chunk, 0, unroll=8)

    def gather(n):
        ref = F[(n + 1) % 2]
        zero = jnp.zeros((NY, REC), f32)

        def one(p, carry):
            hot = rowhot[pl.ds(pl.multiple_of((p + HU) * NY, NY), NY), :].astype(f32)
            parts = []
            for s in range(NS):
                v = jnp.concatenate([ref[1, s, z, p + 1, data, :] for z in range(2)], axis=1)
                parts.extend(split2(v))
            g = jnp.dot(jnp.concatenate(parts, axis=0), zt[...], preferred_element_type=f32)
            return tuple(
                carry[s] + hot * (g[2 * s * NY : (2 * s + 1) * NY] + g[(2 * s + 1) * NY : (2 * s + 2) * NY])
                for s in range(NS)
            )

        got = lax.fori_loop(0, CX, one, (zero, zero), unroll=8)
        for s in range(NS):
            tr[pl.ds(s * STEPS + n, 1), :] = jnp.sum(got[s], axis=0, keepdims=True)

    def inject(kind, lo, hi):
        def plane(i, carry):
            g = (i + CX - HU) // CX
            hot = rowhot[pl.ds(pl.multiple_of(i * NY, NY), NY), :].astype(f32)
            for s in range(NS):
                parts = []
                for n in range(STEPS):
                    v = amt_s[kind, g, pl.ds(s * STEPS + n, 1), :]
                    v_hi = v.astype(bf16).astype(f32)
                    parts.append(
                        jnp.concatenate(
                            [(hot * v_hi).astype(bf16), (hot * (v - v_hi)).astype(bf16)], axis=1
                        )
                    )
                e = jnp.dot(jnp.concatenate(parts, axis=0), zh2[g], preferred_element_type=f32)
                for n in range(STEPS):
                    E[s * STEPS + n, i] = e[n * NY : (n + 1) * NY]
            return carry

        lax.fori_loop(lo, hi, plane, 0, unroll=2)

    def level(m, img):
        now, nxt = U[(m + 1) % 2], U[m % 2]
        n = STEPS - 1 - m

        def plane(image, i, carry):
            q = i - HU

            def chunk(j, inner):
                y8 = pl.multiple_of(j * 8, 8)
                ys = pl.ds(y8, 8)
                ysp = pl.ds(pl.multiple_of(y8 + 8, 8), 8)
                pic = [None, None]
                for s in range(NS):
                    if m > 0:
                        mid, sums = neighbours(now, (s,), i, y8)
                    for z in range(2):
                        zs = pl.ds(z * HALF, HALF)
                        u = inv[z, i, ys, :] * E[s * STEPS + n, i, ys, zs]
                        if m > 0:
                            u = u + (ca[z, i, ys, :] * mid[z] + cc[z, i, ys, :] * sums[z])
                        if m > 1:
                            u = u - cb[z, i, ys, :] * nxt[s, z, i, ysp, :]
                        if m < STEPS - 1:
                            nxt[s, z, i, ysp, :] = u
                        if image:
                            part = band[s, n, q, ys, pl.ds(z * HALF, HALF)] * u
                            pic[z] = part if s == 0 else pic[z] + part
                if image:
                    for z in range(2):
                        zs = pl.ds(z * HALF, HALF)
                        old = 0.0 if m == 0 else img[q, ys, zs]
                        img[q, ys, zs] = old + pic[z]
                return inner

            lax.fori_loop(0, 8, chunk, 0, unroll=8)
            return carry

        if m < STEPS - 1:
            lax.fori_loop(m, HU, functools.partial(plane, False), 0)
            lax.fori_loop(HU + CX, CU - m, functools.partial(plane, False), 0)
        lax.fori_loop(HU, HU + CX, functools.partial(plane, True), 0, unroll=2)

    def edge_bs(n, s):
        def one(k, carry):
            step_bs(n, 1 + (CX - 1) * k, (s,))
            return carry

        lax.fori_loop(0, 2, one, 0, unroll=2)

    def edge_r(n):
        def one(k, carry):
            step_r(n, 1 + (CX - 1) * k)
            return carry

        lax.fori_loop(0, 2, one, 0, unroll=2)

    def inner_bs(n, shots):
        def one(p, carry):
            step_bs(n, p, shots)
            return carry

        lax.fori_loop(2, CX, one, 0, unroll=2)

    def inner_r(n):
        def one(p, carry):
            step_r(n, p)
            return carry

        lax.fori_loop(2, CX, one, 0, unroll=2)

    for n in range(STEPS):
        if n == 0:
            wait_load("bs1")
            inner_bs(n, range(NS))
            wait_load("r1")
            inner_r(n)
        for s in range(NS):
            bs_faces(n, s).wait_recv()
            if n > 0:
                bs_faces(n - 1, s).wait_send()
            edge_bs(n, s)
            if n < STEPS - 1:
                bs_faces(n + 1, s).start()
            if n > 0:
                inner_bs(n, (s,))
        r_faces(n).wait_recv()
        if n > 0:
            r_faces(n - 1).wait_send()
        edge_r(n)
        if n < STEPS - 1:
            r_faces(n + 1).start()
        if n > 0:
            inner_r(n)
        gather(n)
        if n == 0:
            info_halo.wait_recv()
            c_halo.wait_recv()
            for g, lo in ((0, 0), (1, (HU + CX) * NY)):
                hot_rows(info_n[g, pl.ds(8, 1), :], lo, HU * NY)
                hot_z(info_n[g, pl.ds(9, 1), :], 2 * g)
            lax.fori_loop(0, HU, coef, 0)
            lax.fori_loop(HU + CX, CU, coef, 0)
            amt_s[0, 0] = info_n[0, pl.ds(0, 8), :]
            amt_s[0, 1] = info[pl.ds(0, 8), :]
            amt_s[0, 2] = info_n[1, pl.ds(0, 8), :]
            inject(0, 0, CU)
        level(n, img_r)
    for s in range(NS):
        bs_faces(STEPS - 1, s).wait_send()
    r_faces(STEPS - 1).wait_send()
    info_halo.wait_send()
    c_halo.wait_send()

    def to_slabs(r):
        return [
            pltpu.make_async_remote_copy(
                src_ref=ebuf.at[r, 0],
                dst_ref=eslot_g.at[r, me_g],
                send_sem=e_send_g.at[r, d],
                recv_sem=e_recv_g.at[r, d],
                device_id=(me_s, lax.rem(me_g + d, n_gx)),
                device_id_type=MESH,
            )
            for d in range(1, n_gx)
        ]

    def to_shots(r):
        return [
            pltpu.make_async_remote_copy(
                src_ref=ebuf.at[r, 1],
                dst_ref=eslot_s.at[r, me_s],
                send_sem=e_send_s.at[r, d],
                recv_sem=e_recv_s.at[r, d],
                device_id=(lax.rem(me_s + d, n_shot), me_g),
                device_id_type=MESH,
            )
            for d in range(1, n_shot)
        ]

    def sum_start(value, r):
        ebuf[r, 0] = value
        eslot_g[r, me_g] = value
        for c in to_slabs(r):
            c.start()

    def sum_middle(r):
        for c in to_slabs(r):
            c.wait_recv()
        total = eslot_g[r, 0]
        for d in range(1, n_gx):
            total = total + eslot_g[r, d]
        ebuf[r, 1] = total
        eslot_s[r, me_s] = total
        for c in to_shots(r):
            c.start()

    def sum_end(r):
        for c in to_shots(r):
            c.wait_recv()
        total = eslot_s[r, 0]
        for d in range(1, n_shot):
            total = total + eslot_s[r, d]
        return jnp.sum(total)

    t = tr[...]
    tr_halo.start()
    sum_start(t * t, 0)
    amt_s[1, 1] = t
    inject(1, HU, HU + CX)
    tr_halo.wait_recv()
    amt_s[1, 0] = tr_n[0]
    amt_s[1, 2] = tr_n[1]
    inject(1, 0, HU)
    inject(1, HU + CX, CU)
    level(0, img_t)
    sum_middle(0)
    for m in range(1, STEPS - 1):
        level(m, img_t)
    energy = sum_end(0)
    gn = jnp.full((8, HALF), grad_norm[0], f32)
    step = gn / (jnp.full((8, HALF), energy, f32) + tiny)
    for s in range(NS):
        aux_o[pl.ds(s * STEPS, STEPS), :] = (
            residual[s] - step[0:STEPS] * t[s * STEPS : (s + 1) * STEPS]
        )

    def to_sum(d):
        to = lax.rem(me_s + d, n_shot)
        return pltpu.make_async_remote_copy(
            src_ref=img_r.at[to],
            dst_ref=rs.at[d - 1],
            send_sem=g_send.at[0, d],
            recv_sem=g_recv.at[0, d],
            device_id=(to, me_g),
            device_id_type=MESH,
        )

    m_last = STEPS - 1
    now_u, old_u = U[(m_last + 1) % 2], U[m_last % 2]

    def gradient_plane(d, carry):
        q = lax.rem(me_s + d, n_shot)
        i = q + HU

        def chunk(j, inner):
            y8 = pl.multiple_of(j * 8, 8)
            ys = pl.ds(y8, 8)
            ysp = pl.ds(pl.multiple_of(y8 + 8, 8), 8)
            pic = [img_t[q, ys, pl.ds(z * HALF, HALF)] for z in range(2)]
            for s in range(NS):
                mid, sums = neighbours(now_u, (s,), i, y8)
                for z in range(2):
                    zs = pl.ds(z * HALF, HALF)
                    u = inv[z, i, ys, :] * E[s * STEPS, i, ys, zs]
                    u = u + (ca[z, i, ys, :] * mid[z] + cc[z, i, ys, :] * sums[z])
                    u = u - cb[z, i, ys, :] * old_u[s, z, i, ysp, :]
                    pic[z] = pic[z] + band[s, 0, q, ys, zs] * u
            for z in range(2):
                zs = pl.ds(z * HALF, HALF)
                img_r[q, ys, zs] = c0[z, i, ys, :] * (step * pic[z] - img_r[q, ys, zs])
            return inner

        lax.fori_loop(0, 8, chunk, 0, unroll=8)

        @pl.when(d < n_shot)
        def _():
            to_sum(d).start()

        return carry

    lax.fori_loop(1, n_shot + 1, gradient_plane, 0)
    for d in range(1, n_shot):
        to_sum(d).wait_recv()

    def add(i, carry):
        ys = pl.ds(pl.multiple_of(i * 8, 8), 8)
        g = img_r[me_s, ys, :]
        for d in range(1, n_shot):
            g = g + rs[d - 1, ys, :]
        grad_o[me_s, ys, :] = g
        g = g * g
        return carry + (g[:, :HALF] + g[:, HALF:])

    part = lax.fori_loop(0, 8, add, jnp.zeros((8, HALF), f32), unroll=8)
    sum_start(part, 1)
    def spread(d):
        return pltpu.make_async_remote_copy(
            src_ref=grad_o.at[me_s],
            dst_ref=grad_o.at[me_s],
            send_sem=g_send.at[1, d],
            recv_sem=g_recv.at[1, d],
            device_id=(lax.rem(me_s + d, n_shot), me_g),
            device_id_type=MESH,
        )

    for d in range(1, n_shot, 2):
        spread(d).start()
    sum_middle(1)
    for d in range(2, n_shot, 2):
        spread(d).start()
    grad_energy = sum_end(1)
    ratio = jnp.full((8, HALF), grad_energy, f32) / gn
    aux_o[pl.ds(8, 8), :] = step
    aux_o[pl.ds(16, 8), :] = ratio
    for d in range(1, n_shot):
        came = lax.rem(me_s + n_shot - d, n_shot)
        pltpu.make_async_remote_copy(
            src_ref=grad_o.at[came],
            dst_ref=grad_o.at[came],
            send_sem=g_send.at[1, d],
            recv_sem=g_recv.at[1, d],
            device_id=(came, me_g),
            device_id_type=MESH,
        ).wait_recv()
    tr_halo.wait_send()
    for r in range(2):
        for c in to_shots(r) + to_slabs(r):
            c.wait_send()
    for d in range(1, n_shot):
        to_sum(d).wait_send()
        spread(d).wait_send()


def finish(
    aux_h, gradient_h, direction_h, model_h, image_o, dir_o, resid_o,
    aux, gradient, direction, image, resid, sem,
):
    half = CX // 2
    first = pltpu.make_async_copy(aux_h, aux, sem.at[0])
    first.start()
    come = []
    for k in range(2):
        ps = pl.ds(k * half, half)
        for b, (src, dst) in enumerate(
            ((gradient_h, gradient), (direction_h, direction), (model_h, image))
        ):
            c = pltpu.make_async_copy(src.at[ps], dst.at[ps], sem.at[1 + 3 * k + b])
            c.start()
            come.append(c)
    first.wait()
    step = aux[8:9, 0:1]
    ratio = aux[16:17, 0:1]
    for s in range(NS):
        resid[s] = aux[s * STEPS : (s + 1) * STEPS, :]
    gone = [pltpu.make_async_copy(resid, resid_o, sem.at[7])]
    gone[0].start()
    for k in range(2):
        ps = pl.ds(k * half, half)
        for c in come[3 * k : 3 * k + 3]:
            c.wait()

        def plane(p, carry):
            d = direction[p]
            image[p] = image[p] + step * d
            gradient[p] = gradient[p] + ratio * d
            return carry

        lax.fori_loop(k * half, (k + 1) * half, plane, 0)
        for b, (src, dst) in enumerate(((image, image_o), (gradient, dir_o))):
            c = pltpu.make_async_copy(src.at[ps], dst.at[ps], sem.at[8 + 2 * k + b])
            c.start()
            gone.append(c)
    for c in gone:
        c.wait()


def per_device(
    n_shot,
    n_gx,
    courant,
    absorb,
    model_image,
    direction,
    back_prev,
    back_now,
    scat_prev,
    scat_now,
    back_end,
    back_before_end,
    back_band,
    src_pos,
    wavelet,
    rec_pos,
    residual,
    grad_norm,
):
    hbm = pl.BlockSpec(memory_space=pl.ANY)
    vmem = pl.BlockSpec(memory_space=pltpu.VMEM)
    smem = pl.BlockSpec(memory_space=pltpu.SMEM)
    slab = (2, CX, NY, HALF)
    wide = (2, CU, NY, HALF)
    dma = pltpu.SemaphoreType.DMA
    V = pltpu.VMEM
    gradient, aux = pl.pallas_call(
        functools.partial(kernel, n_shot, n_gx),
        out_shape=(
            jax.ShapeDtypeStruct((CX, NY, NZ), f32),
            jax.ShapeDtypeStruct((24, HALF), f32),
        ),
        in_specs=[hbm] * 9 + [smem] * 3 + [vmem] * 3,
        out_specs=(vmem, vmem),
        scratch_shapes=[
            V((2, NS, 2, CX + 2, PY, HALF), f32),
            V((2, NS, 2, CX + 2, PY, HALF), f32),
            V((NS, 2, CX + 2, PY, HALF), f32),
            V((NS, 2, CX + 2, PY, HALF), f32),
            V((NS, 2, CU, PY, HALF), f32),
            V((NS, 2, CU, PY, HALF), f32),
            V((NS, STEPS, CX, NY, NZ), f32),
            V(wide, f32),
            V(slab, f32),
            V(wide, f32),
            V(wide, f32),
            V(wide, f32),
            V(wide, f32),
            V((NS,) + slab, f32),
            V((CU * NY, REC), bf16),
            V((NZ, REC), bf16),
            V((3, 2 * REC, NZ), bf16),
            V((16, REC), f32),
            V((2, 16, REC), f32),
            V((NS * STEPS, REC), f32),
            V((2, NS * STEPS, REC), f32),
            V((2, 3, NS * STEPS, REC), f32),
            V((NS * STEPS, CU, NY, NZ), f32),
            V((CX, NY, NZ), f32),
            V((CX, NY, NZ), f32),
            V((n_shot - 1, NY, NZ), f32),
            V((2, 2, 8, HALF), f32),
            V((2, n_shot, 8, HALF), f32),
            V((2, n_gx, 8, HALF), f32),
            dma((17,)),
            dma((STEPS, NS, 2)),
            dma((STEPS, NS, 2)),
            dma((STEPS, 2)),
            dma((STEPS, 2)),
            dma((3, 2)),
            dma((3, 2)),
            dma((2, n_shot)),
            dma((2, n_shot)),
            dma((2, n_gx)),
            dma((2, n_gx)),
            dma((2, n_shot)),
            dma((2, n_shot)),
        ],
        compiler_params=pltpu.CompilerParams(
            collective_id=0,
            has_side_effects=True,
            vmem_limit_bytes=58 * 1024 * 1024,
        ),
        name="lsrtm",
    )(
        courant,
        direction,
        back_prev,
        back_now,
        scat_prev,
        scat_now,
        back_end,
        back_before_end,
        back_band,
        absorb,
        wavelet,
        grad_norm,
        jnp.transpose(src_pos, (2, 0, 1)),
        jnp.transpose(rec_pos, (2, 0, 1)),
        residual,
    )
    return pl.pallas_call(
        finish,
        out_shape=[
            jax.ShapeDtypeStruct((CX, NY, NZ), f32),
            jax.ShapeDtypeStruct((CX, NY, NZ), f32),
            jax.ShapeDtypeStruct((NS, STEPS, REC), f32),
        ],
        in_specs=[hbm] * 4,
        out_specs=[pl.BlockSpec(memory_space=pltpu.HBM)] * 3,
        scratch_shapes=[
            V((24, HALF), f32),
            V((CX, NY, NZ), f32),
            V((CX, NY, NZ), f32),
            V((CX, NY, NZ), f32),
            V((NS, STEPS, REC), f32),
            dma((12,)),
        ],
        compiler_params=pltpu.CompilerParams(vmem_limit_bytes=62 * 1024 * 1024),
        name="finish",
    )(aux, gradient, direction, model_image)


def solution(mesh):
    field = P("shot", "gx", None, None)
    grid = P("gx", None, None)
    in_specs = (
        grid,
        P(),
        grid,
        grid,
        field,
        field,
        field,
        field,
        field,
        field,
        P("shot", None, "gx", None, None),
        P("shot", None, None),
        P("shot", None),
        P("shot", "gx", None),
        P("shot", None, "gx"),
        P(),
    )
    return jax.shard_map(
        functools.partial(per_device, mesh.shape["shot"], mesh.shape["gx"]),
        mesh=mesh,
        in_specs=in_specs,
        out_specs=(grid, grid, P("shot", None, "gx")),
        check_vma=False,
    )
```
